256 devices in a mesh: tile: 64 (over x, y, z_lo, core), lev: 4 (over z_hi).
Axes of the slice: x: 4, y: 4, z: 8 (z_hi: 4, z_lo: 2; z = z_hi * 2 + z_lo), core: 2. Of those that a mesh axis runs over, the one named last changes fastest.
Arguments:
- tracer: float32 [2, 72, 128, 512], P(None, 'lev', 'tile'), may hold values from -6 to 6
- u_courant: float32 [72, 128, 512], P('lev', 'tile'), may hold values from -0.45 to 0.45
- v_courant: float32 [72, 128, 512], P('lev', 'tile'), may hold values from -0.45 to 0.45
- surface_flux: float32 [2, 128, 512], P(None, 'tile'), may hold values from -6 to 6
- mixing: float32 [72, 72], replicated, may hold values from 0 to 1
- kernel: float32 [72, 262144], P('lev', 'tile'), may hold values from 0.1 to 1
- column: int32 [262144], P('tile'), may hold values from 0 to 1023
- owner_tile: int32 [262144], P('tile'), may hold values from 0 to 63, as said below
- offset: int32 [262144], P('tile'), may hold values from 0 to 23
- counts: int32 [64], P('tile'), may hold values from 2048 to 4096, as said below
Outputs:
- transported: float32 [2, 72, 128, 512], P(None, 'lev', 'tile')
- evolved: float32 [2, 262144], P(None, 'tile')
The draws below stay inside these ranges and needn't reach their ends.
Inputs may be any that keep to these rules, and one draw needn't show every extreme that they name: `owner_tile`: among the rows of one device, no owner tile is named by more than 192 rows; one owner tile, the same for every device, is named by exactly 192 rows of each device. Rows at position counts[t] and beyond in tile t's block of soundings are unused.
All inputs are finite; a program needn't handle non-finite values.
Results may differ from the reference program's by a relative error of at most 0.0003.
Values sent between devices are 32-bit elements; how exact they have to be, the bound alone decides.
No kernel may reach another device: no remote copies, remote signals or barrier semaphores. Data moves between devices by JAX's collectives and lax.ppermute only.
A program may use at most 64 MiB of HBM per device.

```python
import math
import jax
import jax.numpy as jnp
from jax import lax

SCEN = 2
NLEV = 72
LON_DEV = 2
NLAT = 512
NSUB = 2
SND_DEV = 4096
TILES = 64
NLON = 128
SND_TOTAL = 262144
CAP = 192


def draw_mixing(key, part):
    level_ids = jnp.arange(NLEV)
    identity_mask = (level_ids[:, None] == level_ids[None, :]).astype(jnp.float32)
    spread = jax.random.uniform(key, (NLEV, NLEV), jnp.float32)
    return 0.6 * identity_mask + 0.8 / NLEV * spread * (1.0 - identity_mask)


def draw_owner_tile(key, part):
    hot_owner = jax.random.randint(jax.random.fold_in(key, 1), (), 0, TILES)
    remaining = SND_DEV - CAP

    def one_block(block_key):
        first_key, second_key = jax.random.split(block_key)
        chosen = jax.random.permutation(first_key, (TILES - 1) * CAP)[:remaining]
        others = (hot_owner + 1 + chosen // CAP) % TILES
        owners = jnp.concatenate([jnp.full((CAP,), hot_owner, jnp.int32), others.astype(jnp.int32)])
        shuffle = jax.random.permutation(second_key, SND_DEV)
        return owners[shuffle]
    block_keys = jax.random.split(jax.random.fold_in(key, 2), TILES)
    return jax.vmap(one_block)(block_keys).reshape(-1).astype(jnp.int32)


def draw_counts(key, part):
    drawn = jax.random.randint(jax.random.fold_in(key, 3), (TILES,), SND_DEV // 2, SND_DEV + 1)
    full_tile = jax.random.randint(jax.random.fold_in(key, 4), (), 0, TILES)
    tile_ids = jnp.arange(TILES)
    return jnp.where(tile_ids == full_tile, SND_DEV, drawn).astype(jnp.int32)


def set_ends(values, stream_key, smallest, top_value):
    index_at = [jax.random.randint(jax.random.fold_in(stream_key, axis), (), 0, length) for axis, length in enumerate(values.shape)]
    widest = values.shape.index(max(values.shape))
    beside = index_at[:widest] + [(index_at[widest] + 1) % values.shape[widest]] + index_at[widest + 1:]
    return values.at[tuple(index_at)].set(smallest).at[tuple(beside)].set(top_value)


def steps_of(own_key, extent, pieces, least, high):
    def one(position, blocks):
        heights = jax.random.uniform(jax.random.fold_in(jax.random.fold_in(own_key, 6), position), (blocks,), jnp.float32, least / len(pieces), high / len(pieces))
        return jnp.repeat(jnp.exp(heights), extent[position] // blocks).reshape((-1,) + (1,) * (len(extent) - position - 1))

    level = one(*pieces[0])
    for cut in pieces[1:]:
        level = level * one(*cut)
    return level


def centred(own_key, shape, scale, bound, pieces=(), kind=jnp.bfloat16):
    array = scale * jax.random.normal(own_key, shape, jnp.float32)
    if pieces:
        array = array * steps_of(own_key, shape, pieces, -0.22, 0.18)
    return jnp.clip(array, -bound, bound).astype(kind)


def setup_inputs(seed: int = 0) -> dict:
    seeds = jax.random.split(jax.random.key(seed), 11)
    tracer = centred(seeds[0], (SCEN, NLEV, NLON, NLAT), 1.0, 6.0, ((1, 4), (2, 64)), jnp.float32)
    u_courant = jnp.clip(jax.random.uniform(seeds[1], (NLEV, NLON, NLAT), jnp.float32, -0.45, 0.45) * steps_of(seeds[1], (NLEV, NLON, NLAT), ((0, 4), (1, 64)), -0.4, 0.0), -0.45, 0.45)
    v_courant = jnp.clip(jax.random.uniform(seeds[2], (NLEV, NLON, NLAT), jnp.float32, -0.45, 0.45) * steps_of(seeds[2], (NLEV, NLON, NLAT), ((0, 4), (1, 64)), -0.4, 0.0), -0.45, 0.45)
    surface_flux = centred(seeds[3], (SCEN, NLON, NLAT), 1.0, 6.0, ((1, 64),), jnp.float32)
    mixing = draw_mixing(jax.random.fold_in(seeds[10], 71), 0)
    kernel = jnp.clip(jnp.exp(math.log(1.0) - 2.3025851 * jax.random.uniform(seeds[5], (NLEV, SND_TOTAL), jnp.float32) ** steps_of(seeds[5], (NLEV, SND_TOTAL), ((0, 4), (1, 64)), -0.2, 0.2)), 0.1, 1.0)
    column = set_ends(jax.random.randint(seeds[6], (SND_TOTAL,), 0, LON_DEV * NLAT), jax.random.fold_in(seeds[6], 1), 0, (LON_DEV * NLAT) - 1).astype(jnp.int32)
    owner_tile = draw_owner_tile(jax.random.fold_in(seeds[10], 71), 0)
    offset = set_ends(jax.random.randint(seeds[8], (SND_TOTAL,), 0, NLEV // 3), jax.random.fold_in(seeds[8], 1), 0, (NLEV // 3) - 1).astype(jnp.int32)
    counts = draw_counts(jax.random.fold_in(seeds[10], 71), 0)
    return {"tracer": tracer, "u_courant": u_courant, "v_courant": v_courant, "surface_flux": surface_flux, "mixing": mixing, "kernel": kernel, "column": column, "owner_tile": owner_tile, "offset": offset, "counts": counts}


def substep(extended, wind_u, wind_v):
    centre = extended[:, :, 1:-1]
    west_cells = extended[:, :, :-2]
    east_cells = extended[:, :, 2:]
    wind_west = wind_u[:, 1:-1]
    wind_east = wind_u[:, 2:]
    wind_lat = wind_v[:, 1:-1]
    flux_west = wind_west * jnp.where(wind_west > 0, west_cells, centre)
    flux_east = wind_east * jnp.where(wind_east > 0, centre, east_cells)
    south_cells = jnp.concatenate([jnp.zeros_like(centre[..., :1]), centre[..., :-1]], axis=-1)
    lat_ids = lax.broadcasted_iota(jnp.int32, wind_lat.shape, 2)
    open_face = jnp.where(lat_ids > 0, wind_lat, jnp.zeros_like(wind_lat))
    flux_south = open_face * jnp.where(wind_lat > 0, south_cells, centre)
    flux_north = jnp.concatenate([flux_south[..., 1:], jnp.zeros_like(flux_south[..., :1])], axis=-1)
    return centre - (flux_east - flux_west) - (flux_north - flux_south)


def reference(tracer, u_courant, v_courant, surface_flux, mixing, kernel, column, owner_tile, offset, counts):
    advected = tracer.at[:, 0].add(surface_flux)
    winds_u = jnp.concatenate([u_courant[:, -1:], u_courant, u_courant[:, :1]], axis=1)
    winds_v = jnp.concatenate([v_courant[:, -1:], v_courant, v_courant[:, :1]], axis=1)
    for sub_step in range(NSUB):
        extended = jnp.concatenate([advected[:, :, -1:], advected, advected[:, :, :1]], axis=2)
        advected = substep(extended, winds_u, winds_v)
    transported = jnp.einsum("kl,slxy->skxy", mixing, advected, precision=lax.Precision.HIGHEST)
    columns_flat = transported.reshape(SCEN, NLEV, TILES, LON_DEV * NLAT)
    picked = columns_flat[:, :, owner_tile, column]
    level_ids = jnp.arange(NLEV, dtype=jnp.int32)[:, None]
    weighted = jnp.where(level_ids >= offset[None, :], kernel, jnp.zeros_like(kernel))
    sampled = jnp.sum(picked * weighted[None], axis=1)
    denominator = jnp.sum(weighted, axis=0)
    positions = jnp.arange(SND_TOTAL, dtype=jnp.int32)
    in_use = (positions % SND_DEV) < counts[positions // SND_DEV]
    evolved = jnp.where(in_use[None, :], sampled / denominator[None, :], jnp.zeros_like(sampled))
    return transported, evolved
```

```python
import jax
import jax.numpy as jnp
from jax import lax
from jax.experimental import pallas as pl
from jax.experimental.pallas import tpu as pltpu
from jax.sharding import PartitionSpec as P

LANES = 128
SUBS = 8
HERE = 18
ROWS = 24
TILES = 64
CAP = 192
SND = 4096
F32 = jnp.float32
BF16 = jnp.bfloat16
VMEM = pltpu.MemorySpace.VMEM
SMEM = pltpu.MemorySpace.SMEM


def params(mib):
    return pltpu.CompilerParams(vmem_limit_bytes=mib * 2**20)


def spec(space=VMEM):
    return pl.BlockSpec(memory_space=space)


def iota(shape, dim):
    return lax.broadcasted_iota(jnp.int32, shape, dim)


def split(x):
    high = x.astype(BF16)
    low = (x - high.astype(F32)).astype(BF16)
    return high, low


def roll(x, shift, axis):
    return pltpu.roll(x, shift % x.shape[axis], axis)


def swap(x, first):
    return jnp.where(first, roll(x, -1, 0), roll(x, 1, 0))


def inner(c, u, v, first):
    sub, lane = iota(c.shape, 0), iota(c.shape, 1)
    shifted = roll(c, 1, 1)
    south = jnp.where(lane == 0, roll(shifted, 2, 0), shifted)
    wall = (sub < 2) & (lane == 0)
    flux_south = jnp.where(wall, 0.0, v * jnp.where(v > 0, south, c))
    back = roll(flux_south, -1, 1)
    flux_north = jnp.where(lane == LANES - 1, roll(back, -2, 0), back)
    middle = u * jnp.where(u > 0, roll(c, 1, 0), c)
    return c - (flux_north - flux_south) + jnp.where(first, -roll(middle, -1, 0), middle)


def surfaced(c_ref, f_ref, s, level):
    c = c_ref[s * HERE + level]
    ground = (lax.axis_index("lev") == 0) & (level == 0)
    return c + jnp.where(ground, f_ref[s], 0.0)


def halo_kernel(c_ref, u_ref, v_ref, f_ref, east_ref, west_ref, part_ref):
    first = iota((SUBS, LANES), 0) % 2 == 0

    for level in range(HERE):
        u, v = u_ref[level], v_ref[level]
        for s in range(2):
            row = s * HERE + level
            c = c_ref[row]
            if level == 0:
                c = surfaced(c_ref, f_ref, s, level)
            y = inner(c, u, v, first)
            part_ref[row] = y
            east_ref[row] = jnp.where(first, roll(c, -1, 0), y)
            west_ref[row] = jnp.where(first, y, roll(c, 1, 0))
    for level in range(HERE // 2):
        west_ref[2 * HERE + level] = jnp.where(first, u_ref[level], roll(u_ref[level + HERE // 2], 1, 0))


def advect_kernel(c_ref, u_ref, v_ref, f_ref, part_ref, a_ref, b_ref, out_ref):
    first = iota((SUBS, LANES), 0) % 2 == 0
    for level in range(HERE):
        u, v = u_ref[level], v_ref[level]
        packed = b_ref[2 * HERE + level % (HERE // 2)]
        beyond = roll(packed, 1, 0) if level < HERE // 2 else packed
        outer = jnp.where(first, u, beyond)
        forward = outer > 0
        for s in range(2):
            row = s * HERE + level
            c = c_ref[row]
            if level == 0:
                c = surfaced(c_ref, f_ref, s, level)
            a, b = a_ref[row], b_ref[row]
            flux = outer * jnp.where(forward, jnp.where(first, a, c), jnp.where(first, c, b))
            own = part_ref[row] + jnp.where(first, flux, -flux)
            near = swap(jnp.where(first, b + roll(flux, -1, 0), a - roll(flux, 1, 0)), first)
            flux = outer * jnp.where(forward, jnp.where(first, near, own), jnp.where(first, own, near))
            out_ref[row] = inner(own, u, v, first) + jnp.where(first, flux, -flux)


def mix_kernel(mix_ref, x0_ref, x1_ref, x2_ref, x3_ref, out_ref, field_ref):
    z = lax.axis_index("lev")
    refs = (x0_ref, x1_ref, x2_ref, x3_ref)
    cols = [lax.rem(z + d, 4) * HERE for d in range(4)]

    def step(l, acc):
        acc = list(acc)
        for d in range(4):
            xs = [refs[d][s * HERE + l] for s in range(2)]
            for k in range(HERE):
                m = mix_ref[z * HERE + k, cols[d] + l]
                for s in range(2):
                    acc[s * HERE + k] = acc[s * HERE + k] + m * xs[s]
        return tuple(acc)

    zero = jnp.zeros((SUBS, LANES), F32)
    acc = lax.fori_loop(0, HERE, step, (zero,) * (2 * HERE))
    for row in range(2 * HERE):
        out_ref[row] = acc[row]
    for sub in range(SUBS):
        for s in range(2):
            field_ref[sub, s, 0:HERE, :] = out_ref[s * HERE : (s + 1) * HERE, sub, :]
            field_ref[sub, s, HERE:ROWS, :] = jnp.zeros((ROWS - HERE, LANES), F32)


def send_kernel(kern_ref, col_ref, own_ref, off_ref, send_ref, rank_ref, den_ref, w_ref, own8_ref, hot_ref):
    z = lax.axis_index("lev")
    levels = z * HERE + iota((HERE, SND), 0)
    weighted = jnp.where(levels >= off_ref[...], kern_ref[...], 0.0)
    den_ref[...] = jnp.sum(weighted, axis=0, keepdims=True)
    col = col_ref[...].astype(F32)
    w_ref[0:HERE, :] = weighted
    w_ref[HERE : HERE + 1, :] = col
    w_ref[HERE + 1 : HERE + 3, :] = weighted[HERE - 2 : HERE]
    w_ref[HERE + 3 : HERE + 4, :] = col
    w_ref[HERE + 4 : ROWS, :] = jnp.zeros((2, SND), F32)
    own8_ref[...] = jnp.broadcast_to(own_ref[...], (SUBS, SND))

    wide = 256
    before = (iota((wide, wide), 0) < iota((wide, wide), 1)).astype(BF16)
    slot = iota((wide, 1), 0)
    slot = jnp.where(slot < CAP, slot, slot - 64)
    carry = jnp.zeros((TILES, 1), F32)
    for b in range(SND // wide):
        at = pl.ds(b * wide, wide)
        onehot = (iota((TILES, wide), 0) == own_ref[:, at]).astype(F32)
        prefix = jnp.dot(onehot.astype(BF16), before, preferred_element_type=F32)
        rank = jnp.sum(onehot * (prefix + carry), axis=0, keepdims=True).astype(jnp.int32)
        carry = carry + jnp.sum(onehot, axis=1, keepdims=True)
        rank_ref[:, at] = rank
        hot_ref[:, at] = (slot == rank).astype(F32).astype(BF16)

    group, chunk = 8, 1024
    lane = iota((SUBS, LANES), 1)
    sub = iota((SUBS, LANES), 0)

    def some(g, _):
        acc = jnp.zeros((group * ROWS, wide), F32)
        for b in range(SND // chunk):
            at = pl.ds(b * chunk, chunk)
            w = w_ref[:, at]
            high = w.astype(BF16).astype(F32)
            low = w - high
            own = own8_ref[:, at]
            own = jnp.concatenate([own] * 3, axis=0)
            masks = [own == g * group + j for j in range(group)]
            for part in (high, low):
                lhs = jnp.concatenate([jnp.where(m, part, 0.0) for m in masks], axis=0).astype(BF16)
                acc = acc + lax.dot_general(
                    lhs, hot_ref[:, at], (((1,), (1,)), ((), ())), preferred_element_type=F32
                )
        for j in range(group):
            top = acc[j * ROWS : (j + 1) * ROWS, 0:LANES]
            rest = acc[j * ROWS : (j + 1) * ROWS, LANES:]
            t = g * group + j
            send_ref[t, 0:16, :] = top[0:16]
            send_ref[t, 16:24, :] = jnp.where(sub < 3, top[16:24], rest[16:24])
            send_ref[t, 24:32, :] = jnp.where(lane < 64, rest[0:8], rest[8:16])
        return 0

    lax.fori_loop(0, TILES // group, some, 0)


def sample_kernel(got_ref, field_ref, out_ref):
    lane = iota((SUBS, LANES), 1)
    sub = iota((SUBS, LANES), 0)
    left = lane < 64

    def sums(w, colf):
        col = colf.astype(jnp.int32)
        at_lane = jnp.broadcast_to(col & (LANES - 1), (SUBS, LANES))
        at_sub = jnp.broadcast_to(((col >> 7) & 3) * 2 + (col >> 9), (SUBS, LANES))
        totals = []
        hits = [at_sub == k for k in range(SUBS)]
        for s in range(2):
            total = jnp.zeros((SUBS, LANES), F32)
            for g in range(3):
                value = jnp.zeros((SUBS, LANES), F32)
                for k in range(SUBS):
                    rows = field_ref[k, s, 8 * g : 8 * g + 8, :]
                    value = jnp.where(hits[k], jnp.take_along_axis(rows, at_lane, axis=1), value)
                total = total + value * w[g]
            totals.append(jnp.sum(total, axis=0, keepdims=True))
        return totals

    def pair(p, _):
        xs = [[got_ref[2 * p + i, 8 * g : 8 * g + 8, :] for g in range(4)] for i in range(2)]
        full = []
        for x in xs:
            full.append(sums((x[0], x[1], jnp.where(sub < 2, x[2], 0.0)), x[2][2:3]))
        x, y = xs
        last = roll(jnp.where(left, x[2], y[2]), -3, 0)
        rest = sums(
            (
                jnp.where(left, x[3], roll(y[3], 64, 1)),
                jnp.where(left, roll(x[3], 64, 1), y[3]),
                jnp.where(sub < 2, last, 0.0),
            ),
            last[2:3],
        )
        half = lane[0:1] < 64
        tails = (
            jnp.where(half, rest[0], roll(rest[1], 64, 1)),
            jnp.where(half, roll(rest[0], 64, 1), rest[1]),
        )
        for i in range(2):
            out_ref[2 * p + i, 0:1, :] = full[i][0]
            out_ref[2 * p + i, 1:2, :] = full[i][1]
            out_ref[2 * p + i, 2:3, :] = tails[i]
            out_ref[2 * p + i, 3:8, :] = jnp.zeros((5, LANES), F32)
        return 0

    lax.fori_loop(0, TILES // 2, pair, 0)


def home_kernel(back_ref, own_ref, rank_ref, out_ref):
    tail = back_ref[:, 2, :]
    first = jnp.concatenate([back_ref[:, 0, :], tail], axis=1)
    second = jnp.concatenate([back_ref[:, 1, :], roll(tail, 64, 1)], axis=1)
    high, low = split(jnp.concatenate([first, second], axis=0))
    wide = 256
    slot = iota((wide, 1), 0)
    for b in range(SND // wide):
        at = pl.ds(b * wide, wide)
        hot = (slot == rank_ref[:, at]).astype(F32).astype(BF16)
        values = jnp.dot(high, hot, preferred_element_type=F32) + jnp.dot(low, hot, preferred_element_type=F32)
        mine = iota((TILES, wide), 0) == own_ref[:, at]
        for s in range(2):
            picked = jnp.where(mine, values[s * TILES : (s + 1) * TILES], 0.0)
            out_ref[s : s + 1, at] = jnp.sum(picked, axis=0, keepdims=True)


def last_kernel(count_ref, a_ref, b_ref, c_ref, d_ref, da_ref, db_ref, dc_ref, dd_ref, out_ref):
    num = (a_ref[...] + c_ref[...]) + (b_ref[...] + d_ref[...])
    den = (da_ref[...] + dc_ref[...]) + (db_ref[...] + dd_ref[...])
    used = iota((2, SND), 1) < count_ref[0]
    out_ref[...] = jnp.where(used, num / den, 0.0)


def call(kernel, outs, in_specs, scratch=(), mib=12, flops=10**6, name=None):
    single = not isinstance(outs, (list, tuple))
    shapes = [outs] if single else outs
    return pl.pallas_call(
        kernel,
        out_shape=outs if single else list(outs),
        in_specs=in_specs,
        out_specs=spec() if single else [spec() for _ in shapes],
        scratch_shapes=list(scratch),
        compiler_params=params(mib),
        name=name,
        cost_estimate=pl.CostEstimate(flops=flops, bytes_accessed=10**5, transcendentals=0),
    )


def arr(shape, dtype=F32):
    return jax.ShapeDtypeStruct(shape, dtype)


def registers(x):
    rows = x.size // (SUBS * LANES)
    return x.reshape(rows, 2, 4, LANES).transpose(0, 2, 1, 3).reshape(rows, SUBS, LANES)


def shift(x, axis, distance):
    size = lax.axis_size(axis)
    return lax.ppermute(x, axis, [(i, (i + distance) % size) for i in range(size)])


def body(tracer, u_courant, v_courant, surface_flux, mixing, kernel, column, owner_tile, offset, counts):
    c, u, v, f = (registers(x) for x in (tracer, u_courant, v_courant, surface_flux))
    col, own, off = (x.reshape(1, SND) for x in (column, owner_tile, offset))
    east, west, part = call(
        halo_kernel, [arr((36, SUBS, LANES)), arr((45, SUBS, LANES)), arr((36, SUBS, LANES))], [spec()] * 4, name="halo"
    )(c, u, v, f)
    from_west = shift(east, "tile", 1)
    from_east = shift(west, "tile", -1)
    send, rank, den = call(
        send_kernel,
        [arr((TILES, 32, LANES)), arr((1, SND), jnp.int32), arr((1, SND))],
        [spec()] * 4,
        [pltpu.VMEM((ROWS, SND), F32), pltpu.VMEM((SUBS, SND), jnp.int32), pltpu.VMEM((256, SND), BF16)],
        mib=24,
        flops=10**9,
        name="send",
    )(kernel, col, own, off)
    got = lax.all_to_all(send, "tile", 0, 0, tiled=True)
    adv = call(advect_kernel, arr((36, SUBS, LANES)), [spec()] * 7, name="advect")(c, u, v, f, part, from_west, from_east)
    others = [shift(adv, "lev", -d) for d in (1, 2, 3)]
    dens = [shift(den, "lev", -d) for d in (1, 2, 3)]
    transported, field = call(
        mix_kernel,
        [arr((36, SUBS, LANES)), arr((SUBS, 2, ROWS, LANES))],
        [spec(SMEM)] + [spec()] * 4,
        name="mix",
    )(mixing, adv, *others)
    sums = call(sample_kernel, arr((TILES, SUBS, LANES)), [spec()] * 2, name="sample")(got, field)
    back = lax.all_to_all(sums, "tile", 0, 0, tiled=True)
    mine = call(home_kernel, arr((2, SND)), [spec()] * 3, name="home")(back, own, rank)
    nums = [shift(mine, "lev", -d) for d in (1, 2, 3)]
    evolved = call(last_kernel, arr((2, SND)), [spec(SMEM)] + [spec()] * 8, name="last")(
        counts, mine, *nums, den, *dens
    )
    out = transported.reshape(36, 4, 2, LANES).transpose(0, 2, 1, 3).reshape(tracer.shape)
    return out, evolved


def solution(mesh):
    in_specs = (
        P(None, "lev", "tile", None),
        P("lev", "tile", None),
        P("lev", "tile", None),
        P(None, "tile", None),
        P(),
        P("lev", "tile"),
        P("tile"),
        P("tile"),
        P("tile"),
        P("tile"),
    )
    out_specs = (P(None, "lev", "tile", None), P(None, "tile"))
    return jax.shard_map(body, mesh=mesh, in_specs=in_specs, out_specs=out_specs, check_vma=False)
```

```python
import jax
import jax.numpy as jnp
from jax import lax
from jax.experimental import pallas as pl
from jax.experimental.pallas import tpu as pltpu
from jax.sharding import PartitionSpec as P

LANES = 128
SUBS = 8
HERE = 18
ROWS = 24
TILES = 64
WIDE = 256
QUADS = 4
SND = 4096
F32 = jnp.float32
BF16 = jnp.bfloat16
VMEM = pltpu.MemorySpace.VMEM
SMEM = pltpu.MemorySpace.SMEM
HBM = pltpu.MemorySpace.HBM


def params(mib):
    return pltpu.CompilerParams(vmem_limit_bytes=mib * 2**20)


def spec(space=VMEM):
    return pl.BlockSpec(memory_space=space)


def iota(shape, dim):
    return lax.broadcasted_iota(jnp.int32, shape, dim)


def split(x):
    high = x.astype(BF16)
    low = (x - high.astype(F32)).astype(BF16)
    return high, low


def roll(x, shift, axis):
    return pltpu.roll(x, shift % x.shape[axis], axis)


def swap(x, first):
    return jnp.where(first, roll(x, -1, 0), roll(x, 1, 0))


def inner(c, u, v, first):
    sub, lane = iota(c.shape, 0), iota(c.shape, 1)
    shifted = roll(c, 1, 1)
    south = jnp.where(lane == 0, roll(shifted, 2, 0), shifted)
    wall = (sub < 2) & (lane == 0)
    flux_south = jnp.where(wall, 0.0, v * jnp.where(v > 0, south, c))
    back = roll(flux_south, -1, 1)
    flux_north = jnp.where(lane == LANES - 1, roll(back, -2, 0), back)
    middle = u * jnp.where(u > 0, roll(c, 1, 0), c)
    return c - (flux_north - flux_south) + jnp.where(first, -roll(middle, -1, 0), middle)


def surfaced(c_ref, f_ref, s, level):
    c = c_ref[s * HERE + level]
    if level > 0:
        return c
    return c + jnp.where(lax.axis_index("lev") == 0, f_ref[s], 0.0)


def halo_kernel(c_in, u_in, v_in, f_in, east_ref, west_ref, part_ref, c_ref, u_ref, v_ref, f_ref, sem):
    fetch(((c_in, c_ref), (u_in, u_ref), (v_in, v_ref), (f_in, f_ref)), sem)
    first = iota((SUBS, LANES), 0) % 2 == 0
    for level in range(HERE):
        u, v = u_ref[level], v_ref[level]
        for s in range(2):
            row = s * HERE + level
            c = surfaced(c_ref, f_ref, s, level)
            y = inner(c, u, v, first)
            part_ref[row] = y
            east_ref[row] = jnp.where(first, roll(c, -1, 0), y)
            west_ref[row] = jnp.where(first, y, roll(c, 1, 0))
    for level in range(HERE // 2):
        west_ref[2 * HERE + level] = jnp.where(first, u_ref[level], roll(u_ref[level + HERE // 2], 1, 0))


def advect_kernel(c_ref, u_ref, v_ref, f_ref, part_ref, a_ref, b_ref, den_ref, out_ref):
    first = iota((SUBS, LANES), 0) % 2 == 0
    for level in range(HERE):
        u, v = u_ref[level], v_ref[level]
        packed = b_ref[2 * HERE + level % (HERE // 2)]
        beyond = roll(packed, 1, 0) if level < HERE // 2 else packed
        outer = jnp.where(first, u, beyond)
        forward = outer > 0
        for s in range(2):
            row = s * HERE + level
            c = surfaced(c_ref, f_ref, s, level)
            a, b = a_ref[row], b_ref[row]
            flux = outer * jnp.where(forward, jnp.where(first, a, c), jnp.where(first, c, b))
            own = part_ref[row] + jnp.where(first, flux, -flux)
            near = swap(jnp.where(first, b + roll(flux, -1, 0), a - roll(flux, 1, 0)), first)
            flux = outer * jnp.where(forward, jnp.where(first, near, own), jnp.where(first, own, near))
            out_ref[row] = inner(own, u, v, first) + jnp.where(first, flux, -flux)
    for row in range(4):
        out_ref[2 * HERE + row] = den_ref[row]


def mix_kernel(mix_ref, x0_ref, x1_ref, x2_ref, x3_ref, out_ref, field_ref, den_ref):
    refs = (x0_ref, x1_ref, x2_ref, x3_ref)
    high, low = split(mix_ref[...])
    both = jnp.concatenate([high.astype(F32), low.astype(F32)], axis=0).astype(BF16)
    pad = jnp.zeros((ROWS - HERE, 2 * LANES), F32)
    for s in range(2):
        rows = slice(s * HERE, (s + 1) * HERE)
        for sub in range(0, SUBS, 2):
            parts = []
            for ref in refs:
                parts += [jnp.concatenate([ref[rows, sub, :], ref[rows, sub + 1, :]], axis=1), pad]
            x_high, x_low = split(jnp.concatenate(parts, axis=0))
            r = jnp.dot(both, x_high, preferred_element_type=F32)
            mixed = r[0:ROWS] + r[ROWS:] + jnp.dot(high, x_low, preferred_element_type=F32)
            for i in range(2):
                half = mixed[:, i * LANES : (i + 1) * LANES]
                field_ref[sub + i, s] = half
                out_ref[rows, sub + i, :] = half[0:HERE]
    for row in range(4):
        a, b, c, d = (ref[2 * HERE + row] for ref in refs)
        den_ref[row] = (a + c) + (b + d)


def place(own, rank):
    full = rank < LANES
    group = (own >> 2) * 3 + jnp.where(full, (own & 3) >> 1, 2)
    lane = jnp.where(full, (own & 1) * LANES + rank, (own & 3) * 64 + rank - LANES)
    return group, lane


def fetch(pairs, sem):
    copies = [pltpu.make_async_copy(a, b, sem.at[i]) for i, (a, b) in enumerate(pairs)]
    for copy in copies:
        copy.start()
    for copy in copies:
        copy.wait()


def send_kernel(
    kern_in, col_in, own_in, off_in, part_ref, send_ref, rank_ref, den_ref,
    kern_ref, col_ref, own_ref, off_ref, w_ref, grp_ref, hot_ref, sem,
):
    fetch(((kern_in, kern_ref), (col_in, col_ref), (own_in, own_ref), (off_in, off_ref)), sem)
    z = lax.axis_index("lev")
    levels = z * HERE + iota((HERE, SND), 0)
    weighted = jnp.where(levels >= off_ref[...], kern_ref[...], 0.0)
    den = jnp.sum(weighted, axis=0, keepdims=True)
    for j in range(SND // LANES):
        den_ref[j // SUBS, j % SUBS : j % SUBS + 1, :] = den[:, j * LANES : (j + 1) * LANES]
    col = col_ref[...].astype(F32)
    w_ref[0:HERE, :] = weighted
    w_ref[HERE : HERE + 1, :] = col
    w_ref[HERE + 1 : HERE + 3, :] = weighted[HERE - 2 : HERE]
    w_ref[HERE + 3 : HERE + 4, :] = col
    w_ref[HERE + 4 : ROWS, :] = jnp.zeros((2, SND), F32)

    before = (iota((WIDE, WIDE), 0) < iota((WIDE, WIDE), 1)).astype(BF16)
    slot = iota((WIDE, 1), 0)
    carry = jnp.zeros((TILES, 1), F32)
    for b in range(SND // WIDE):
        at = pl.ds(b * WIDE, WIDE)
        own = own_ref[:, at]
        onehot = (iota((TILES, WIDE), 0) == own).astype(F32)
        prefix = jnp.dot(onehot.astype(BF16), before, preferred_element_type=F32)
        rank = jnp.sum(onehot * (prefix + carry), axis=0, keepdims=True).astype(jnp.int32)
        carry = carry + jnp.sum(onehot, axis=1, keepdims=True)
        rank_ref[:, at] = rank
        group, lane = place(own, rank)
        grp_ref[:, at] = jnp.broadcast_to(group, (SUBS, WIDE))
        hot_ref[at, :] = (slot == lane).astype(F32).T.astype(BF16)

    quads, chunk = 8, 1024
    sub, left = iota((SUBS, LANES), 0), iota((SUBS, LANES), 1) < 64

    def some(i, _):
        acc = jnp.zeros((quads * 3 * 2 * ROWS, WIDE), F32)
        for b in range(SND // chunk):
            at = pl.ds(b * chunk, chunk)
            w = w_ref[:, at]
            high = w.astype(BF16).astype(F32)
            low = w - high
            group = jnp.concatenate([grp_ref[:, at]] * 3, axis=0)
            rows = []
            for j in range(quads * 3):
                here = group == i * quads * 3 + j
                rows += [jnp.where(here, high, 0.0), jnp.where(here, low, 0.0)]
            lhs = jnp.concatenate(rows, axis=0).astype(BF16)
            acc = acc + jnp.dot(lhs, hot_ref[at, :], preferred_element_type=F32)
        for q in range(quads):
            sums = []
            for j in range(3):
                base = (q * 3 + j) * 2 * ROWS
                sums.append(acc[base : base + ROWS] + acc[base + ROWS : base + 2 * ROWS])
            for k in range(4):
                t = (i * quads + q) * 4 + k
                top = sums[k // 2][:, (k % 2) * LANES : (k % 2 + 1) * LANES]
                rest = sums[2][:, (k // 2) * LANES : (k // 2 + 1) * LANES]
                middle = rest[16:24]
                if k % 2 == 0:
                    bottom = jnp.where(left, rest[0:8], roll(rest[8:16], 64, 1))
                else:
                    bottom = jnp.where(left, roll(rest[0:8], 64, 1), rest[8:16])
                    middle = roll(middle, 64, 1)
                send_ref[t, 0:16, :] = top[0:16]
                send_ref[t, 16:24, :] = jnp.where(sub < 3, top[16:24], middle)
                send_ref[t, 24:32, :] = bottom
        return 0

    lax.fori_loop(0, TILES // (4 * quads), some, 0)


FIELD = 40


def sample_kernel(got_ref, field_ref, out_ref, f_ref):
    sub, lane = iota((SUBS, LANES), 0), iota((SUBS, LANES), 1)
    left = lane < 64
    for h in range(4):
        blocks = []
        for lon in range(2):
            x, y = field_ref[2 * h + lon, 0], field_ref[2 * h + lon, 1]
            third = jnp.where(sub < 2, x[16:24], roll(y[16:24], 3, 0))
            blocks.append(jnp.concatenate([x[0:16], y[0:16], third], axis=0))
        high, low = split(jnp.concatenate(blocks, axis=1))
        f_ref[h * FIELD : (h + 1) * FIELD, :] = high
        f_ref[(4 + h) * FIELD : (5 + h) * FIELD, :] = low
    spot = iota((WIDE, 1), 0)
    row = iota((SUBS, WIDE), 0)

    def sums(w, col):
        col = col.astype(jnp.int32)
        hot = (spot == (col & 127) + ((col >> 9) << 7)).astype(F32).astype(BF16)
        block = jnp.broadcast_to((col >> 7) & 3, (SUBS, WIDE))
        hits = [block == h for h in range(4)]
        both = jnp.dot(f_ref[...], hot, preferred_element_type=F32)
        values = both[0 : 4 * FIELD] + both[4 * FIELD :]

        def pick(base):
            out = values[base : base + 8]
            for h in range(1, 4):
                out = jnp.where(hits[h], values[h * FIELD + base : h * FIELD + base + 8], out)
            return out

        last = jnp.where(row < 2, w[2], 0.0)
        last = pick(32) * (last + roll(last, 3, 0))
        totals = []
        for s in range(2):
            total = pick(16 * s) * w[0] + pick(16 * s + 8) * w[1] + jnp.where((row < 3) == (s == 0), last, 0.0)
            totals.append(jnp.sum(total, axis=0, keepdims=True))
        return totals

    def wide(a, b):
        return jnp.concatenate([a, b], axis=1)

    quads = QUADS
    half = lane[0:1] < 64

    def some(i, _):
        rows = ([], [], [])
        for q in range(quads):
            t = (i * quads + q) * 4
            xs = [[got_ref[t + k, 8 * g : 8 * g + 8, :] for g in range(4)] for k in range(4)]
            results, rest = [], []
            for x, y in (xs[0:2], xs[2:4]):
                w = [wide(x[g], y[g]) for g in range(3)]
                results.append(sums(w, w[2][2:3]))
                rest.append(
                    (
                        jnp.where(left, x[3], roll(y[3], 64, 1)),
                        jnp.where(left, roll(x[3], 64, 1), y[3]),
                        roll(jnp.where(left, x[2], roll(y[2], 64, 1)), -3, 0),
                    )
                )
            w = [wide(rest[0][g], rest[1][g]) for g in range(3)]
            tails = sums(w, w[2][2:3])
            for k in range(4):
                mine = slice((k % 2) * LANES, (k % 2 + 1) * LANES)
                pair = slice((k // 2) * LANES, (k // 2 + 1) * LANES)
                a, b = tails[0][:, pair], tails[1][:, pair]
                tail = jnp.where(half, a, roll(b, 64, 1)) if k % 2 == 0 else jnp.where(half, roll(a, 64, 1), b)
                for j, x in enumerate((results[k // 2][0][:, mine], results[k // 2][1][:, mine], tail)):
                    rows[j].append(x)
        at = pl.ds(pl.multiple_of(i * 4 * quads, 4 * quads), 4 * quads)
        for j in range(3):
            out_ref[at, j * LANES : (j + 1) * LANES] = jnp.concatenate(rows[j], axis=0)
        return 0

    lax.fori_loop(0, TILES // (4 * quads), some, 0)


def home_kernel(back_ref, own_ref, rank_ref, out_ref):
    tail = back_ref[:, 2 * LANES : 3 * LANES]
    first = jnp.concatenate([back_ref[:, 0:LANES], tail], axis=1)
    second = jnp.concatenate([back_ref[:, LANES : 2 * LANES], roll(tail, 64, 1)], axis=1)
    high, low = split(jnp.concatenate([first, second], axis=0))
    slot = iota((WIDE, 1), 0)
    for b in range(SND // WIDE):
        at = pl.ds(b * WIDE, WIDE)
        hot = (slot == rank_ref[:, at]).astype(F32).astype(BF16)
        values = jnp.dot(high, hot, preferred_element_type=F32) + jnp.dot(low, hot, preferred_element_type=F32)
        mine = iota((TILES, WIDE), 0) == own_ref[:, at]
        for s in range(2):
            picked = jnp.where(mine, values[s * TILES : (s + 1) * TILES], 0.0)
            total = jnp.sum(picked, axis=0, keepdims=True)
            for i in range(2):
                j = s * 32 + 2 * b + i
                out_ref[j // SUBS, j % SUBS : j % SUBS + 1, :] = total[:, i * LANES : (i + 1) * LANES]


def last_kernel(count_ref, a_ref, b_ref, c_ref, d_ref, den_ref, out_ref):
    count = count_ref[0]
    for row in range(4):
        number = (row * SUBS + iota((SUBS, LANES), 0)) * LANES + iota((SUBS, LANES), 1)
        den = den_ref[row]
        for s in range(2):
            k = s * 4 + row
            num = (a_ref[k] + c_ref[k]) + (b_ref[k] + d_ref[k])
            value = jnp.where(number < count, num / den, 0.0)
            for j in range(SUBS):
                at = (row * SUBS + j) * LANES
                out_ref[s : s + 1, at : at + LANES] = value[j : j + 1]


def call(kernel, outs, in_specs, scratch=(), mib=12, flops=10**6, name=None):
    single = not isinstance(outs, (list, tuple))
    shapes = [outs] if single else outs
    return pl.pallas_call(
        kernel,
        out_shape=outs if single else list(outs),
        in_specs=in_specs,
        out_specs=spec() if single else [spec() for _ in shapes],
        scratch_shapes=list(scratch),
        compiler_params=params(mib),
        name=name,
        cost_estimate=pl.CostEstimate(flops=flops, bytes_accessed=10**5, transcendentals=0),
    )


def arr(shape, dtype=F32):
    return jax.ShapeDtypeStruct(shape, dtype)


def registers(x):
    rows = x.size // (SUBS * LANES)
    return x.reshape(rows, 2, 4, LANES).transpose(0, 2, 1, 3).reshape(rows, SUBS, LANES)


def far(x):
    return pltpu.with_memory_space_constraint(x, HBM)


def shift(x, axis, distance):
    size = lax.axis_size(axis)
    return lax.ppermute(x, axis, [(i, (i + distance) % size) for i in range(size)])


def body(tracer, u_courant, v_courant, surface_flux, mixing, kernel, column, owner_tile, offset, counts):
    c, u, v, f = (registers(x) for x in (tracer, u_courant, v_courant, surface_flux))
    col, own, off = (x.reshape(1, SND) for x in (column, owner_tile, offset))
    block = arr((2 * HERE, SUBS, LANES))
    east, west, part = call(
        halo_kernel,
        [block, arr((45, SUBS, LANES)), block],
        [spec(HBM)] * 4,
        [
            pltpu.VMEM((2 * HERE, SUBS, LANES), F32),
            pltpu.VMEM((HERE, SUBS, LANES), F32),
            pltpu.VMEM((HERE, SUBS, LANES), F32),
            pltpu.VMEM((2, SUBS, LANES), F32),
            pltpu.SemaphoreType.DMA((4,)),
        ],
        name="halo",
    )(*(far(x) for x in (c, u, v, f)))
    from_west = shift(east, "tile", 1)
    from_east = shift(west, "tile", -1)
    send, rank, den = call(
        send_kernel,
        [arr((TILES, 32, LANES)), arr((1, SND), jnp.int32), arr((4, SUBS, LANES))],
        [spec(HBM)] * 4 + [spec()],
        [pltpu.VMEM((HERE, SND), F32)]
        + [pltpu.VMEM((1, SND), jnp.int32)] * 3
        + [pltpu.VMEM((ROWS, SND), F32), pltpu.VMEM((SUBS, SND), jnp.int32), pltpu.VMEM((SND, WIDE), BF16), pltpu.SemaphoreType.DMA((4,))],
        mib=28,
        flops=9 * 10**9,
        name="send",
    )(*(far(x) for x in (kernel, col, own, off)), part)
    send, from_west, from_east = lax.optimization_barrier((send, from_west, from_east))
    got = lax.all_to_all(send, "tile", 0, 0, tiled=True)
    adv = call(advect_kernel, arr((40, SUBS, LANES)), [spec()] * 8, name="advect")(
        c, u, v, f, part, from_west, from_east, den
    )
    others = [shift(adv, "lev", -d) for d in (1, 2, 3)]
    first = lax.axis_index("lev") * HERE
    twice = jnp.concatenate([mixing, mixing], axis=1)
    rows = lax.dynamic_slice(twice, (first, first), (HERE, 4 * HERE)).reshape(HERE, 4, HERE)
    rows = jnp.pad(rows, ((0, ROWS - HERE), (0, 0), (0, ROWS - HERE))).reshape(ROWS, 4 * ROWS)
    transported, field, weight = call(
        mix_kernel,
        [block, arr((SUBS, 2, ROWS, LANES)), arr((4, SUBS, LANES))],
        [spec()] * 5,
        name="mix",
    )(rows, adv, *others)
    sums = call(
        sample_kernel,
        arr((TILES, 3 * LANES)),
        [spec()] * 2,
        [pltpu.VMEM((8 * FIELD, WIDE), BF16)],
        mib=24,
        name="sample",
    )(got, field)
    back = lax.all_to_all(sums, "tile", 0, 0, tiled=True)
    mine = call(home_kernel, arr((8, SUBS, LANES)), [spec()] * 3, name="home")(back, own, rank)
    nums = [shift(mine, "lev", -d) for d in (1, 2, 3)]
    evolved = call(last_kernel, arr((2, SND)), [spec(SMEM)] + [spec()] * 5, name="last")(counts, mine, *nums, weight)
    out = transported.reshape(2 * HERE, 4, 2, LANES).transpose(0, 2, 1, 3).reshape(tracer.shape)
    return out, evolved


def solution(mesh):
    in_specs = (
        P(None, "lev", "tile", None),
        P("lev", "tile", None),
        P("lev", "tile", None),
        P(None, "tile", None),
        P(),
        P("lev", "tile"),
        P("tile"),
        P("tile"),
        P("tile"),
        P("tile"),
    )
    out_specs = (P(None, "lev", "tile", None), P(None, "tile"))
    return jax.shard_map(body, mesh=mesh, in_specs=in_specs, out_specs=out_specs, check_vma=False)
```

```python
import jax
import jax.numpy as jnp
from jax import lax
from jax.experimental import pallas as pl
from jax.experimental.pallas import tpu as pltpu
from jax.sharding import PartitionSpec as P

LANES = 128
SUBS = 8
HERE = 18
ROWS = 24
TILES = 64
WIDE = 256
QUADS = 8
ORDER = "H"
MARK = 1000000
MIX = 100000000000
RELAY = False
SND = 4096
F32 = jnp.float32
BF16 = jnp.bfloat16
VMEM = pltpu.MemorySpace.VMEM
SMEM = pltpu.MemorySpace.SMEM
HBM = pltpu.MemorySpace.HBM


def params(mib):
    return pltpu.CompilerParams(vmem_limit_bytes=mib * 2**20)


def spec(space=VMEM):
    return pl.BlockSpec(memory_space=space)


def iota(shape, dim):
    return lax.broadcasted_iota(jnp.int32, shape, dim)


def split(x):
    high = x.astype(BF16)
    low = (x - high.astype(F32)).astype(BF16)
    return high, low


def roll(x, shift, axis):
    return pltpu.roll(x, shift % x.shape[axis], axis)


def swap(x, first):
    return jnp.where(first, roll(x, -1, 0), roll(x, 1, 0))


def inner(c, u, v, first):
    sub, lane = iota(c.shape, 0), iota(c.shape, 1)
    shifted = roll(c, 1, 1)
    south = jnp.where(lane == 0, roll(shifted, 2, 0), shifted)
    wall = (sub < 2) & (lane == 0)
    flux_south = jnp.where(wall, 0.0, v * jnp.where(v > 0, south, c))
    back = roll(flux_south, -1, 1)
    flux_north = jnp.where(lane == LANES - 1, roll(back, -2, 0), back)
    middle = u * jnp.where(u > 0, roll(c, 1, 0), c)
    return c - (flux_north - flux_south) + jnp.where(first, -roll(middle, -1, 0), middle)


def surfaced(c_ref, f_ref, s, level):
    c = c_ref[s * HERE + level]
    if level > 0:
        return c
    return c + jnp.where(lax.axis_index("lev") == 0, f_ref[s], 0.0)


def halo_kernel(c_in, u_in, v_in, f_in, near_ref, far_ref, part_ref, c_ref, u_ref, v_ref, f_ref, sem):
    fetch(((c_in, c_ref), (u_in, u_ref), (v_in, v_ref), (f_in, f_ref)), sem)
    first = iota((SUBS, LANES), 0) % 2 == 0
    even = lax.axis_index("tile") % 2 == 0
    for level in range(HERE):
        u, v = u_ref[level], v_ref[level]
        for s in range(2):
            row = s * HERE + level
            c = surfaced(c_ref, f_ref, s, level)
            y = inner(c, u, v, first)
            part_ref[row] = y
            east = jnp.where(first, roll(c, -1, 0), y)
            west = jnp.where(first, y, roll(c, 1, 0))
            near_ref[row] = jnp.where(even, east, west)
            far_ref[row] = jnp.where(even, west, east)
    for level in range(HERE // 2):
        u = jnp.where(first, u_ref[level], roll(u_ref[level + HERE // 2], 1, 0))
        near_ref[2 * HERE + level] = u
        far_ref[2 * HERE + level] = u


def advect_kernel(c_ref, u_ref, v_ref, f_ref, part_ref, near_ref, far_ref, den_ref, out_ref):
    even = lax.axis_index("tile") % 2 == 0
    first = iota((SUBS, LANES), 0) % 2 == 0
    for level in range(HERE):
        u, v = u_ref[level], v_ref[level]
        row = 2 * HERE + level % (HERE // 2)
        packed = jnp.where(even, near_ref[row], far_ref[row])
        beyond = roll(packed, 1, 0) if level < HERE // 2 else packed
        outer = jnp.where(first, u, beyond)
        forward = outer > 0
        for s in range(2):
            row = s * HERE + level
            c = surfaced(c_ref, f_ref, s, level)
            a = jnp.where(even, far_ref[row], near_ref[row])
            b = jnp.where(even, near_ref[row], far_ref[row])
            flux = outer * jnp.where(forward, jnp.where(first, a, c), jnp.where(first, c, b))
            own = part_ref[row] + jnp.where(first, flux, -flux)
            near = swap(jnp.where(first, b + roll(flux, -1, 0), a - roll(flux, 1, 0)), first)
            flux = outer * jnp.where(forward, jnp.where(first, near, own), jnp.where(first, own, near))
            out_ref[row] = inner(own, u, v, first) + jnp.where(first, flux, -flux)
    for row in range(4):
        out_ref[2 * HERE + row] = den_ref[row]


def mark_kernel(x_ref, out_ref):
    out_ref[...] = x_ref[0]


def mix_kernel(mix_ref, mark_ref, *refs):
    *refs, out_ref, field_ref, den_ref = refs
    size = 2 * HERE + 4

    def block(d, row, count, sub):
        if d == 2 and len(refs) == 5:
            lower, upper = refs[2:4]
            cut = size // 2
            parts = []
            if row < cut:
                parts.append(lower[row : min(row + count, cut), sub, :])
            if row + count > cut:
                parts.append(upper[max(row - cut, 0) : row + count - cut, sub, :])
            return parts[0] if len(parts) == 1 else jnp.concatenate(parts, axis=0)
        return refs[d if d < 3 else -1][row : row + count, sub, :]

    def weights(d, row):
        if d == 2 and len(refs) == 5:
            return refs[3][row - size // 2]
        return refs[d if d < 3 else -1][row]

    high, low = split(mix_ref[...])
    both = jnp.concatenate([high.astype(F32), low.astype(F32)], axis=0).astype(BF16)
    pad = jnp.zeros((ROWS - HERE, 2 * LANES), F32)
    for s in range(2):
        rows = slice(s * HERE, (s + 1) * HERE)
        for sub in range(0, SUBS, 2):
            parts = []
            for d in range(4):
                parts += [jnp.concatenate([block(d, s * HERE, HERE, sub + i) for i in range(2)], axis=1), pad]
            x_high, x_low = split(jnp.concatenate(parts, axis=0))
            r = jnp.dot(both, x_high, preferred_element_type=F32)
            mixed = r[0:ROWS] + r[ROWS:] + jnp.dot(high, x_low, preferred_element_type=F32)
            for i in range(2):
                half = mixed[:, i * LANES : (i + 1) * LANES]
                field_ref[sub + i, s] = half
                out_ref[rows, sub + i, :] = half[0:HERE]
    for row in range(4):
        a, b, c, d = (weights(i, 2 * HERE + row) for i in range(4))
        den_ref[row] = (a + c) + (b + d)


def place(own, rank):
    full = rank < LANES
    group = (own >> 2) * 3 + jnp.where(full, (own & 3) >> 1, 2)
    lane = jnp.where(full, (own & 1) * LANES + rank, (own & 3) * 64 + rank - LANES)
    return group, lane


def fetch(pairs, sem, needed=None):
    copies = [pltpu.make_async_copy(a, b, sem.at[i]) for i, (a, b) in enumerate(pairs)]
    for copy in copies:
        copy.start()
    for copy in copies[:needed]:
        copy.wait()
    return copies[needed:] if needed else []


BOTH = 40


def send_kernel(
    kern_in, col_in, own_in, off_in, part_ref, send_ref, place_ref, den_ref,
    kern_ref, col_ref, own_ref, off_ref, w_ref, grp_ref, hot_ref, sem,
):
    rest = fetch(((own_in, own_ref), (off_in, off_ref), (col_in, col_ref), (kern_in, kern_ref)), sem, 1)
    before = (iota((WIDE, WIDE), 0) < iota((WIDE, WIDE), 1)).astype(BF16)
    slot = iota((WIDE, 1), 0)
    carry = jnp.zeros((TILES, 1), F32)
    for b in range(SND // WIDE):
        at = pl.ds(b * WIDE, WIDE)
        own = own_ref[:, at]
        onehot = (iota((TILES, WIDE), 0) == own).astype(F32)
        prefix = jnp.dot(onehot.astype(BF16), before, preferred_element_type=F32)
        rank = jnp.sum(onehot * (prefix + carry), axis=0, keepdims=True).astype(jnp.int32)
        carry = carry + jnp.sum(onehot, axis=1, keepdims=True)
        place_ref[:, at] = own * WIDE + rank
        group, lane = place(own, rank)
        grp_ref[:, at] = jnp.broadcast_to(group, (SUBS, WIDE))
        hot_ref[at, :] = (slot == lane).astype(F32).T.astype(BF16)

    for copy in rest:
        copy.wait()
    z = lax.axis_index("lev")
    levels = z * HERE + iota((HERE, SND), 0)
    weighted = jnp.where(levels >= off_ref[...], kern_ref[...], 0.0)
    den = jnp.sum(weighted, axis=0, keepdims=True)
    for j in range(SND // LANES):
        den_ref[j // SUBS, j % SUBS : j % SUBS + 1, :] = den[:, j * LANES : (j + 1) * LANES]
    col = col_ref[...]
    high = weighted.astype(BF16).astype(F32)
    col_high = (col & ~3).astype(F32)
    last = slice(HERE - 2, HERE)
    w_ref[0:16, :] = high[0:16]
    w_ref[16:32, :] = (weighted - high)[0:16]
    w_ref[32:34, :] = high[last]
    w_ref[34:35, :] = col_high
    w_ref[35:37, :] = (weighted - high)[last]
    w_ref[37:38, :] = (col & 3).astype(F32)
    w_ref[38:40, :] = jnp.zeros((2, SND), F32)

    quads, chunk = 16, 512
    sub, left = iota((SUBS, LANES), 0), iota((SUBS, LANES), 1) < 64

    def some(i, _):
        acc = jnp.zeros((quads * 3 * BOTH, WIDE), F32)
        for b in range(SND // chunk):
            at = pl.ds(b * chunk, chunk)
            w = w_ref[:, at]
            group = grp_ref[:, at]
            rows = []
            for j in range(quads * 3):
                here = group == i * quads * 3 + j
                rows += [jnp.where(here, w[k : k + SUBS], 0.0) for k in range(0, BOTH, SUBS)]
            lhs = jnp.concatenate(rows, axis=0).astype(BF16)
            acc = acc + jnp.dot(lhs, hot_ref[at, :], preferred_element_type=F32)
        for q in range(quads):
            sums = []
            for j in range(3):
                base = (q * 3 + j) * BOTH
                third = acc[base + 32 : base + 40]
                third = third + roll(third, 3 if j == 2 else -3, 0)
                sums.append((acc[base : base + 16] + acc[base + 16 : base + 32], third))
            for k in range(4):
                t = (i * quads + q) * 4 + k
                mine = slice((k % 2) * LANES, (k % 2 + 1) * LANES)
                pair = slice((k // 2) * LANES, (k // 2 + 1) * LANES)
                top, third = (x[:, mine] for x in sums[k // 2])
                rest, middle = (x[:, pair] for x in sums[2])
                if k % 2 == 0:
                    bottom = jnp.where(left, rest[0:8], roll(rest[8:16], 64, 1))
                else:
                    bottom = jnp.where(left, roll(rest[0:8], 64, 1), rest[8:16])
                    middle = roll(middle, 64, 1)
                send_ref[t, 0:16, :] = top
                send_ref[t, 16:24, :] = jnp.where(sub < 3, third, jnp.where(sub < 6, middle, 0.0))
                send_ref[t, 24:32, :] = bottom
        return 0

    lax.fori_loop(0, TILES // (4 * quads), some, 0)


FIELD = 40


def sample_kernel(got_ref, field_ref, out_ref, f_ref):
    sub, lane = iota((SUBS, LANES), 0), iota((SUBS, LANES), 1)
    left = lane < 64
    for h in range(4):
        blocks = []
        for lon in range(2):
            x, y = field_ref[2 * h + lon, 0], field_ref[2 * h + lon, 1]
            third = jnp.where(sub < 2, x[16:24], roll(y[16:24], 3, 0))
            blocks.append(jnp.concatenate([x[0:16], y[0:16], third], axis=0))
        high, low = split(jnp.concatenate(blocks, axis=1))
        f_ref[h * FIELD : (h + 1) * FIELD, :] = high
        f_ref[(4 + h) * FIELD : (5 + h) * FIELD, :] = low
    spot = iota((WIDE, 1), 0)
    row = iota((SUBS, WIDE), 0)

    def sums(w, col):
        col = col.astype(jnp.int32)
        hot = (spot == (col & 127) + ((col >> 9) << 7)).astype(F32).astype(BF16)
        block = jnp.broadcast_to((col >> 7) & 3, (SUBS, WIDE))
        hits = [block == h for h in range(4)]
        both = jnp.dot(f_ref[...], hot, preferred_element_type=F32)
        values = both[0 : 4 * FIELD] + both[4 * FIELD :]

        def pick(base):
            out = values[base : base + 8]
            for h in range(1, 4):
                out = jnp.where(hits[h], values[h * FIELD + base : h * FIELD + base + 8], out)
            return out

        last = jnp.where(row < 2, w[2], 0.0)
        last = pick(32) * (last + roll(last, 3, 0))
        totals = []
        for s in range(2):
            total = pick(16 * s) * w[0] + pick(16 * s + 8) * w[1] + jnp.where((row < 3) == (s == 0), last, 0.0)
            totals.append(jnp.sum(total, axis=0, keepdims=True))
        return totals

    def wide(a, b):
        return jnp.concatenate([a, b], axis=1)

    quads = QUADS
    half = lane[0:1] < 64

    def some(i, _):
        rows = ([], [], [])
        for q in range(quads):
            t = (i * quads + q) * 4
            xs = [[got_ref[t + k, 8 * g : 8 * g + 8, :] for g in range(4)] for k in range(4)]
            results, rest = [], []
            for x, y in (xs[0:2], xs[2:4]):
                w = [wide(x[g], y[g]) for g in range(3)]
                results.append(sums(w, w[2][2:3]))
                rest.append(
                    (
                        jnp.where(left, x[3], roll(y[3], 64, 1)),
                        jnp.where(left, roll(x[3], 64, 1), y[3]),
                        roll(jnp.where(left, x[2], roll(y[2], 64, 1)), -3, 0),
                    )
                )
            w = [wide(rest[0][g], rest[1][g]) for g in range(3)]
            tails = sums(w, w[2][2:3])
            for k in range(4):
                mine = slice((k % 2) * LANES, (k % 2 + 1) * LANES)
                pair = slice((k // 2) * LANES, (k // 2 + 1) * LANES)
                a, b = tails[0][:, pair], tails[1][:, pair]
                tail = jnp.where(half, a, roll(b, 64, 1)) if k % 2 == 0 else jnp.where(half, roll(a, 64, 1), b)
                for j, x in enumerate((results[k // 2][0][:, mine], results[k // 2][1][:, mine], tail)):
                    rows[j].append(x)
        at = pl.ds(pl.multiple_of(i * 4 * quads, 4 * quads), 4 * quads)
        for j in range(3):
            out_ref[at, j * LANES : (j + 1) * LANES] = jnp.concatenate(rows[j], axis=0)
        return 0

    lax.fori_loop(0, TILES // (4 * quads), some, 0)


def home_kernel(back_ref, place_ref, out_ref):
    tail = back_ref[:, 2 * LANES : 3 * LANES]
    first = jnp.concatenate([back_ref[:, 0:LANES], tail], axis=1)
    second = jnp.concatenate([back_ref[:, LANES : 2 * LANES], roll(tail, 64, 1)], axis=1)
    high, low = split(jnp.concatenate([first, second], axis=0))
    slot = iota((WIDE, 1), 0)
    for b in range(SND // WIDE):
        at = pl.ds(b * WIDE, WIDE)
        hot = (slot == (place_ref[:, at] & (WIDE - 1))).astype(F32).astype(BF16)
        values = jnp.dot(high, hot, preferred_element_type=F32) + jnp.dot(low, hot, preferred_element_type=F32)
        mine = iota((TILES, WIDE), 0) == (place_ref[:, at] >> 8)
        for s in range(2):
            picked = jnp.where(mine, values[s * TILES : (s + 1) * TILES], 0.0)
            total = jnp.sum(picked, axis=0, keepdims=True)
            for i in range(2):
                j = s * 32 + 2 * b + i
                out_ref[j // SUBS, j % SUBS : j % SUBS + 1, :] = total[:, i * LANES : (i + 1) * LANES]


def last_kernel(count_ref, a_ref, b_ref, c_ref, d_ref, den_ref, out_ref):
    count = count_ref[0]
    for row in range(4):
        number = (row * SUBS + iota((SUBS, LANES), 0)) * LANES + iota((SUBS, LANES), 1)
        den = den_ref[row]
        for s in range(2):
            k = s * 4 + row
            num = (a_ref[k] + c_ref[k]) + (b_ref[k] + d_ref[k])
            value = jnp.where(number < count, num / den, 0.0)
            for j in range(SUBS):
                at = (row * SUBS + j) * LANES
                out_ref[s : s + 1, at : at + LANES] = value[j : j + 1]


def call(kernel, outs, in_specs, scratch=(), mib=12, flops=10**6, name=None):
    single = not isinstance(outs, (list, tuple))
    shapes = [outs] if single else outs
    return pl.pallas_call(
        kernel,
        out_shape=outs if single else list(outs),
        in_specs=in_specs,
        out_specs=spec() if single else [spec() for _ in shapes],
        scratch_shapes=list(scratch),
        compiler_params=params(mib),
        name=name,
        cost_estimate=pl.CostEstimate(flops=flops, bytes_accessed=10**5, transcendentals=0),
    )


def arr(shape, dtype=F32):
    return jax.ShapeDtypeStruct(shape, dtype)


def registers(x):
    rows = x.size // (SUBS * LANES)
    return x.reshape(rows, 2, 4, LANES).transpose(0, 2, 1, 3).reshape(rows, SUBS, LANES)


def swapped(x, start):
    size = lax.axis_size("tile")
    pairs = [((i + start) % size, (i + start + 1) % size) for i in range(0, size, 2)]
    return lax.ppermute(x, "tile", pairs + [(b, a) for a, b in pairs])


def far(x):
    return pltpu.with_memory_space_constraint(x, HBM)


def shift(x, axis, distance):
    size = lax.axis_size(axis)
    return lax.ppermute(x, axis, [(i, (i + distance) % size) for i in range(size)])


def body(tracer, u_courant, v_courant, surface_flux, mixing, kernel, column, owner_tile, offset, counts):
    c, u, v, f = (registers(x) for x in (tracer, u_courant, v_courant, surface_flux))
    col, own, off = (x.reshape(1, SND) for x in (column, owner_tile, offset))
    block = arr((2 * HERE, SUBS, LANES))
    near_half, far_half, part = call(
        halo_kernel,
        [arr((45, SUBS, LANES)), arr((45, SUBS, LANES)), block],
        [spec(HBM)] * 4,
        [
            pltpu.VMEM((2 * HERE, SUBS, LANES), F32),
            pltpu.VMEM((HERE, SUBS, LANES), F32),
            pltpu.VMEM((HERE, SUBS, LANES), F32),
            pltpu.VMEM((2, SUBS, LANES), F32),
            pltpu.SemaphoreType.DMA((4,)),
        ],
        name="halo",
    )(*(far(x) for x in (c, u, v, f)))
    from_near, from_far = swapped(near_half, 0), swapped(far_half, 1)
    send, place_of, den = call(
        send_kernel,
        [arr((TILES, 32, LANES)), arr((1, SND), jnp.int32), arr((4, SUBS, LANES))],
        [spec(HBM)] * 4 + [spec()],
        [pltpu.VMEM((HERE, SND), F32)]
        + [pltpu.VMEM((1, SND), jnp.int32)] * 3
        + [pltpu.VMEM((BOTH, SND), F32), pltpu.VMEM((SUBS, SND), jnp.int32), pltpu.VMEM((SND, WIDE), BF16), pltpu.SemaphoreType.DMA((4,))],
        mib=28,
        flops=9 * 10**9,
        name="send",
    )(*(far(x) for x in (kernel, col, own, off)), part)
    if ORDER == "A":
        send, from_west, from_east = lax.optimization_barrier((send, from_west, from_east))
        got = lax.all_to_all(send, "tile", 0, 0, tiled=True)
    adv = call(advect_kernel, arr((40, SUBS, LANES)), [spec()] * 8, name="advect")(
        c, u, v, f, part, from_near, from_far, den
    )
    up, down = shift(adv, "lev", -1), shift(adv, "lev", 1)
    if ORDER == "B":
        send, adv = lax.optimization_barrier((send, adv))
        got = lax.all_to_all(send, "tile", 0, 0, tiled=True)
    if ORDER == "C":
        send, up = lax.optimization_barrier((send, up))
        got = lax.all_to_all(send, "tile", 0, 0, tiled=True)
    if ORDER == "H":
        mark = call(mark_kernel, arr((SUBS, LANES)), [spec()], flops=MARK, name="mark")(adv)
        send, mark = lax.optimization_barrier((send, mark))
        got = lax.all_to_all(send, "tile", 0, 0, tiled=True)
    if RELAY:
        across = [shift(up[:20], "lev", -1), shift(down[20:], "lev", 1)]
    else:
        across = [shift(adv, "lev", 2)]
    if ORDER == "D":
        send, *across = lax.optimization_barrier((send, *across))
        got = lax.all_to_all(send, "tile", 0, 0, tiled=True)
    first = lax.axis_index("lev") * HERE
    twice = jnp.concatenate([mixing, mixing], axis=1)
    rows = lax.dynamic_slice(twice, (first, first), (HERE, 4 * HERE)).reshape(HERE, 4, HERE)
    rows = jnp.pad(rows, ((0, ROWS - HERE), (0, 0), (0, ROWS - HERE))).reshape(ROWS, 4 * ROWS)
    transported, field, weight = call(
        mix_kernel,
        [block, arr((SUBS, 2, ROWS, LANES)), arr((4, SUBS, LANES))],
        [spec()] * (5 + len(across)),
        flops=MIX,
        name="mix",
    )(rows, mark, adv, up, *across, down)
    sums = call(
        sample_kernel,
        arr((TILES, 3 * LANES)),
        [spec()] * 2,
        [pltpu.VMEM((8 * FIELD, WIDE), BF16)],
        mib=24,
        name="sample",
    )(got, field)
    back = lax.all_to_all(sums, "tile", 0, 0, tiled=True)
    mine = call(home_kernel, arr((8, SUBS, LANES)), [spec()] * 2, name="home")(back, place_of)
    nums = [shift(mine, "lev", -d) for d in (1, 2, 3)]
    evolved = call(last_kernel, arr((2, SND)), [spec(SMEM)] + [spec()] * 5, name="last")(counts, mine, *nums, weight)
    out = transported.reshape(2 * HERE, 4, 2, LANES).transpose(0, 2, 1, 3).reshape(tracer.shape)
    return out, evolved


def solution(mesh):
    in_specs = (
        P(None, "lev", "tile", None),
        P("lev", "tile", None),
        P("lev", "tile", None),
        P(None, "tile", None),
        P(),
        P("lev", "tile"),
        P("tile"),
        P("tile"),
        P("tile"),
        P("tile"),
    )
    out_specs = (P(None, "lev", "tile", None), P(None, "tile"))
    return jax.shard_map(body, mesh=mesh, in_specs=in_specs, out_specs=out_specs, check_vma=False)
```

```python
import jax
import jax.numpy as jnp
from jax import lax
from jax.experimental import pallas as pl
from jax.experimental.pallas import tpu as pltpu
from jax.sharding import PartitionSpec as P

LANES = 128
SUBS = 8
HERE = 18
ROWS = 24
TILES = 64
WIDE = 256
QUADS = 8
SND = 4096
F32 = jnp.float32
BF16 = jnp.bfloat16
VMEM = pltpu.MemorySpace.VMEM
SMEM = pltpu.MemorySpace.SMEM
HBM = pltpu.MemorySpace.HBM


def params(mib):
    return pltpu.CompilerParams(vmem_limit_bytes=mib * 2**20)


def spec(space=VMEM):
    return pl.BlockSpec(memory_space=space)


def iota(shape, dim):
    return lax.broadcasted_iota(jnp.int32, shape, dim)


def split(x):
    high = x.astype(BF16)
    low = (x - high.astype(F32)).astype(BF16)
    return high, low


def roll(x, shift, axis):
    return pltpu.roll(x, shift % x.shape[axis], axis)


def swap(x, first):
    return jnp.where(first, roll(x, -1, 0), roll(x, 1, 0))


def inner(c, u, v, first):
    sub, lane = iota(c.shape, 0), iota(c.shape, 1)
    shifted = roll(c, 1, 1)
    south = jnp.where(lane == 0, roll(shifted, 2, 0), shifted)
    wall = (sub < 2) & (lane == 0)
    flux_south = jnp.where(wall, 0.0, v * jnp.where(v > 0, south, c))
    back = roll(flux_south, -1, 1)
    flux_north = jnp.where(lane == LANES - 1, roll(back, -2, 0), back)
    middle = u * jnp.where(u > 0, roll(c, 1, 0), c)
    return c - (flux_north - flux_south) + jnp.where(first, -roll(middle, -1, 0), middle)


def surfaced(c_ref, f_ref, s, level):
    c = c_ref[s * HERE + level]
    if level > 0:
        return c
    return c + jnp.where(lax.axis_index("lev") == 0, f_ref[s], 0.0)


def halo_kernel(c_in, u_in, v_in, f_in, near_ref, far_ref, part_ref, c_ref, u_ref, v_ref, f_ref, sem):
    fetch(((c_in, c_ref), (u_in, u_ref), (v_in, v_ref), (f_in, f_ref)), sem)
    first = iota((SUBS, LANES), 0) % 2 == 0
    even = lax.axis_index("tile") % 2 == 0
    for level in range(HERE):
        u, v = u_ref[level], v_ref[level]
        for s in range(2):
            row = s * HERE + level
            c = surfaced(c_ref, f_ref, s, level)
            y = inner(c, u, v, first)
            part_ref[row] = y
            east = jnp.where(first, roll(c, -1, 0), y)
            west = jnp.where(first, y, roll(c, 1, 0))
            near_ref[row] = jnp.where(even, east, west)
            far_ref[row] = jnp.where(even, west, east)
    for level in range(HERE // 2):
        u = jnp.where(first, u_ref[level], roll(u_ref[level + HERE // 2], 1, 0))
        near_ref[2 * HERE + level] = u
        far_ref[2 * HERE + level] = u


def advect_kernel(c_ref, u_ref, v_ref, f_ref, part_ref, near_ref, far_ref, den_ref, out_ref):
    even = lax.axis_index("tile") % 2 == 0
    first = iota((SUBS, LANES), 0) % 2 == 0
    for level in range(HERE):
        u, v = u_ref[level], v_ref[level]
        row = 2 * HERE + level % (HERE // 2)
        packed = jnp.where(even, near_ref[row], far_ref[row])
        beyond = roll(packed, 1, 0) if level < HERE // 2 else packed
        outer = jnp.where(first, u, beyond)
        forward = outer > 0
        for s in range(2):
            row = s * HERE + level
            c = surfaced(c_ref, f_ref, s, level)
            a = jnp.where(even, far_ref[row], near_ref[row])
            b = jnp.where(even, near_ref[row], far_ref[row])
            flux = outer * jnp.where(forward, jnp.where(first, a, c), jnp.where(first, c, b))
            own = part_ref[row] + jnp.where(first, flux, -flux)
            near = swap(jnp.where(first, b + roll(flux, -1, 0), a - roll(flux, 1, 0)), first)
            flux = outer * jnp.where(forward, jnp.where(first, near, own), jnp.where(first, own, near))
            out_ref[row] = inner(own, u, v, first) + jnp.where(first, flux, -flux)
    for row in range(4):
        out_ref[2 * HERE + row] = den_ref[row]


def mark_kernel(x_ref, out_ref):
    out_ref[...] = x_ref[0]


def mix_kernel(mix_ref, mark_ref, *refs):
    *refs, out_ref, field_ref, den_ref = refs
    size = 2 * HERE + 4

    def block(d, row, count, sub):
        if d == 2 and len(refs) == 5:
            lower, upper = refs[2:4]
            cut = size // 2
            parts = []
            if row < cut:
                parts.append(lower[row : min(row + count, cut), sub, :])
            if row + count > cut:
                parts.append(upper[max(row - cut, 0) : row + count - cut, sub, :])
            return parts[0] if len(parts) == 1 else jnp.concatenate(parts, axis=0)
        return refs[d if d < 3 else -1][row : row + count, sub, :]

    def weights(d, row):
        if d == 2 and len(refs) == 5:
            return refs[3][row - size // 2]
        return refs[d if d < 3 else -1][row]

    z = lax.axis_index("lev")
    level = iota((ROWS, 4 * HERE), 0)
    pick = ((iota((ROWS, 4 * HERE), 1) == z * HERE + level) & (level < HERE)).astype(F32).astype(BF16)
    at = iota((4 * HERE, 4 * ROWS), 1)
    turn = (at >= ROWS).astype(jnp.int32) + (at >= 2 * ROWS).astype(jnp.int32) + (at >= 3 * ROWS).astype(jnp.int32)
    level = at - turn * ROWS
    source = ((z + turn) & 3) * HERE + level
    spread = ((iota((4 * HERE, 4 * ROWS), 0) == source) & (level < HERE)).astype(F32).astype(BF16)

    def chosen(part):
        rows = jnp.dot(pick, part, preferred_element_type=F32).astype(BF16)
        return jnp.dot(rows, spread, preferred_element_type=F32).astype(BF16)

    high, low = (chosen(part) for part in split(mix_ref[...]))
    both = jnp.concatenate([high.astype(F32), low.astype(F32)], axis=0).astype(BF16)
    pad = jnp.zeros((ROWS - HERE, 2 * LANES), F32)
    for s in range(2):
        rows = slice(s * HERE, (s + 1) * HERE)
        for sub in range(0, SUBS, 2):
            parts = []
            for d in range(4):
                parts += [jnp.concatenate([block(d, s * HERE, HERE, sub + i) for i in range(2)], axis=1), pad]
            x_high, x_low = split(jnp.concatenate(parts, axis=0))
            r = jnp.dot(both, x_high, preferred_element_type=F32)
            mixed = r[0:ROWS] + r[ROWS:] + jnp.dot(high, x_low, preferred_element_type=F32)
            for i in range(2):
                half = mixed[:, i * LANES : (i + 1) * LANES]
                field_ref[sub + i, s] = half
                out_ref[rows, sub + i, :] = half[0:HERE]
    for row in range(4):
        a, b, c, d = (weights(i, 2 * HERE + row) for i in range(4))
        den_ref[row] = (a + c) + (b + d)


def place(own, rank):
    full = rank < LANES
    group = (own >> 2) * 3 + jnp.where(full, (own & 3) >> 1, 2)
    lane = jnp.where(full, (own & 1) * LANES + rank, (own & 3) * 64 + rank - LANES)
    return group, lane


def fetch(pairs, sem):
    copies = [pltpu.make_async_copy(a, b, sem.at[i]) for i, (a, b) in enumerate(pairs)]
    for copy in copies:
        copy.start()
    for copy in copies:
        copy.wait()


MESSAGE = 29
BOTH = 40


def send_kernel(
    kern_in, col_ref, own_ref, off_ref, part_ref, send_ref, place_ref, den_ref,
    kern_ref, w_ref, grp_ref, hot_ref, sem,
):
    weights = pltpu.make_async_copy(kern_in, kern_ref, sem)
    weights.start()
    before = (iota((WIDE, WIDE), 0) < iota((WIDE, WIDE), 1)).astype(BF16)
    slot = iota((WIDE, 1), 0)
    carry = jnp.zeros((TILES, 1), F32)
    for b in range(SND // WIDE):
        at = pl.ds(b * WIDE, WIDE)
        own = own_ref[:, at]
        onehot = (iota((TILES, WIDE), 0) == own).astype(F32)
        prefix = jnp.dot(onehot.astype(BF16), before, preferred_element_type=F32)
        rank = jnp.sum(onehot * (prefix + carry), axis=0, keepdims=True).astype(jnp.int32)
        carry = carry + jnp.sum(onehot, axis=1, keepdims=True)
        place_ref[:, at] = own * WIDE + rank
        group, lane = place(own, rank)
        grp_ref[:, at] = jnp.broadcast_to(group, (SUBS, WIDE))
        hot_ref[at, :] = (slot == lane).astype(F32).T.astype(BF16)

    weights.wait()
    z = lax.axis_index("lev")
    levels = z * HERE + iota((HERE, SND), 0)
    weighted = jnp.where(levels >= off_ref[...], kern_ref[...], 0.0)
    den = jnp.sum(weighted, axis=0, keepdims=True)
    for j in range(SND // LANES):
        den_ref[j // SUBS, j % SUBS : j % SUBS + 1, :] = den[:, j * LANES : (j + 1) * LANES]
    col = col_ref[...]
    high = weighted.astype(BF16).astype(F32)
    col_high = (col & ~3).astype(F32)
    last = slice(HERE - 2, HERE)
    w_ref[0:16, :] = high[0:16]
    w_ref[16:32, :] = (weighted - high)[0:16]
    w_ref[32:34, :] = high[last]
    w_ref[34:35, :] = col_high
    w_ref[35:37, :] = (weighted - high)[last]
    w_ref[37:38, :] = (col & 3).astype(F32)
    w_ref[38:40, :] = jnp.zeros((2, SND), F32)

    quads, chunk = 16, 512
    sub, left = iota((SUBS, LANES), 0), iota((SUBS, LANES), 1) < 64

    def some(i):
        acc = jnp.zeros((quads * 3 * BOTH, WIDE), F32)
        for b in range(SND // chunk):
            at = pl.ds(b * chunk, chunk)
            w = w_ref[:, at]
            group = grp_ref[:, at]
            rows = []
            for j in range(quads * 3):
                here = group == i * quads * 3 + j
                rows += [jnp.where(here, w[k : k + SUBS], 0.0) for k in range(0, BOTH, SUBS)]
            lhs = jnp.concatenate(rows, axis=0).astype(BF16)
            acc = acc + jnp.dot(lhs, hot_ref[at, :], preferred_element_type=F32)
        for q in range(quads):
            sums = []
            for j in range(3):
                base = (q * 3 + j) * BOTH
                third = acc[base + 32 : base + 40]
                third = third + roll(third, 3 if j == 2 else -3, 0)
                sums.append((acc[base : base + 16] + acc[base + 16 : base + 32], third))
            for k in range(4):
                t = (i * quads + q) * 4 + k
                mine = slice((k % 2) * LANES, (k % 2 + 1) * LANES)
                pair = slice((k // 2) * LANES, (k // 2 + 1) * LANES)
                top, third = (x[:, mine] for x in sums[k // 2])
                rest, middle = (x[:, pair] for x in sums[2])
                if k % 2 == 0:
                    bottom = jnp.where(left, rest[0:8], roll(rest[8:16], 64, 1))
                else:
                    bottom = jnp.where(left, roll(rest[0:8], 64, 1), rest[8:16])
                    middle = roll(middle, 64, 1)
                send_ref[MESSAGE * t : MESSAGE * t + 16, :] = top
                send_ref[MESSAGE * t + 16 : MESSAGE * t + 24, :] = bottom
                after = roll(middle, -1, 0)
                split_row = jnp.where(left, middle, roll(after, 64, 1))
                tail = jnp.where(sub < 3, third, jnp.where(sub == 3, split_row, after))
                send_ref[MESSAGE * t + 24 : MESSAGE * t + 29, :] = tail[0:5]

    for i in range(TILES // (4 * quads)):
        some(i)


FIELD = 40


def sample_kernel(got_ref, field_ref, out_ref, f_ref):
    sub, lane = iota((SUBS, LANES), 0), iota((SUBS, LANES), 1)
    left = lane < 64
    for h in range(4):
        blocks = []
        for lon in range(2):
            x, y = field_ref[2 * h + lon, 0], field_ref[2 * h + lon, 1]
            third = jnp.where(sub < 2, x[16:24], roll(y[16:24], 3, 0))
            blocks.append(jnp.concatenate([x[0:16], y[0:16], third], axis=0))
        high, low = split(jnp.concatenate(blocks, axis=1))
        f_ref[h * FIELD : (h + 1) * FIELD, :] = high
        f_ref[(4 + h) * FIELD : (5 + h) * FIELD, :] = low
    spot = iota((WIDE, 1), 0)
    row = iota((SUBS, WIDE), 0)

    def sums(w, col):
        col = col.astype(jnp.int32)
        hot = (spot == (col & 127) + ((col >> 9) << 7)).astype(F32).astype(BF16)
        block = jnp.broadcast_to((col >> 7) & 3, (SUBS, WIDE))
        hits = [block == h for h in range(4)]
        both = jnp.dot(f_ref[...], hot, preferred_element_type=F32)
        values = both[0 : 4 * FIELD] + both[4 * FIELD :]

        def pick(base):
            out = values[base : base + 8]
            for h in range(1, 4):
                out = jnp.where(hits[h], values[h * FIELD + base : h * FIELD + base + 8], out)
            return out

        last = jnp.where(row < 2, w[2], 0.0)
        last = pick(32) * (last + roll(last, 3, 0))
        totals = []
        for s in range(2):
            total = pick(16 * s) * w[0] + pick(16 * s + 8) * w[1] + jnp.where((row < 3) == (s == 0), last, 0.0)
            totals.append(jnp.sum(total, axis=0, keepdims=True))
        return totals

    def wide(a, b):
        return jnp.concatenate([a, b], axis=1)

    def last_of(x, y):
        a = jnp.where(left, x, roll(y, 64, 1))
        b = jnp.where(left, roll(x, 64, 1), y)
        return jnp.where(sub == 0, roll(a, -3, 0), jnp.where(sub == 1, roll(b, -2, 0), roll(a, -2, 0)))

    quads = QUADS
    half = lane[0:1] < 64

    def some(i, _):
        rows = []
        step = 4 * quads * MESSAGE
        got = got_ref.at[pl.ds(pl.multiple_of(i * step, SUBS), step)]
        for q in range(quads):
            xs = []
            for k in range(4):
                base = (q * 4 + k) * MESSAGE
                tail = jnp.concatenate([got[base + 24 : base + 29, :], jnp.zeros((3, LANES), F32)], axis=0)
                xs.append([got[base : base + 8, :], got[base + 8 : base + 16, :], tail, got[base + 16 : base + 24, :]])
            results, rest = [], []
            for x, y in (xs[0:2], xs[2:4]):
                w = [wide(x[g], y[g]) for g in range(3)]
                results.append(sums(w, w[2][2:3]))
                rest.append(
                    (
                        jnp.where(left, x[3], roll(y[3], 64, 1)),
                        jnp.where(left, roll(x[3], 64, 1), y[3]),
                        last_of(x[2], y[2]),
                    )
                )
            w = [wide(rest[0][g], rest[1][g]) for g in range(3)]
            tails = sums(w, w[2][2:3])
            for k in range(4):
                mine = slice((k % 2) * LANES, (k % 2 + 1) * LANES)
                pair = slice((k // 2) * LANES, (k // 2 + 1) * LANES)
                a, b = tails[0][:, pair], tails[1][:, pair]
                tail = jnp.where(half, a, roll(b, 64, 1)) if k % 2 == 0 else jnp.where(half, roll(a, 64, 1), b)
                rows += [results[k // 2][0][:, mine], results[k // 2][1][:, mine], tail]
        size = 12 * quads
        out_ref[pl.ds(pl.multiple_of(i * size, SUBS), size), :] = jnp.concatenate(rows, axis=0)
        return 0

    lax.fori_loop(0, TILES // (4 * quads), some, 0)


def home_kernel(back_ref, place_ref, out_ref):
    plain, other, tail = (back_ref[pl.ds(j, TILES, stride=3), :] for j in range(3))
    first = jnp.concatenate([plain, tail], axis=1)
    second = jnp.concatenate([other, roll(tail, 64, 1)], axis=1)
    high, low = split(jnp.concatenate([first, second], axis=0))
    slot = iota((WIDE, 1), 0)
    for b in range(SND // WIDE):
        at = pl.ds(b * WIDE, WIDE)
        hot = (slot == (place_ref[:, at] & (WIDE - 1))).astype(F32).astype(BF16)
        values = jnp.dot(high, hot, preferred_element_type=F32) + jnp.dot(low, hot, preferred_element_type=F32)
        mine = iota((TILES, WIDE), 0) == (place_ref[:, at] >> 8)
        for s in range(2):
            picked = jnp.where(mine, values[s * TILES : (s + 1) * TILES], 0.0)
            total = jnp.sum(picked, axis=0, keepdims=True)
            for i in range(2):
                j = s * 32 + 2 * b + i
                out_ref[j // SUBS, j % SUBS : j % SUBS + 1, :] = total[:, i * LANES : (i + 1) * LANES]


def last_kernel(count_ref, a_ref, b_ref, c_ref, d_ref, den_ref, out_ref):
    count = count_ref[0]
    for row in range(4):
        number = (row * SUBS + iota((SUBS, LANES), 0)) * LANES + iota((SUBS, LANES), 1)
        den = den_ref[row]
        for s in range(2):
            k = s * 4 + row
            num = (a_ref[k] + c_ref[k]) + (b_ref[k] + d_ref[k])
            value = jnp.where(number < count, num / den, 0.0)
            for j in range(SUBS):
                at = (row * SUBS + j) * LANES
                out_ref[s : s + 1, at : at + LANES] = value[j : j + 1]


def call(kernel, outs, in_specs, scratch=(), mib=12, flops=10**6, name=None):
    single = not isinstance(outs, (list, tuple))
    shapes = [outs] if single else outs
    return pl.pallas_call(
        kernel,
        out_shape=outs if single else list(outs),
        in_specs=in_specs,
        out_specs=spec() if single else [spec() for _ in shapes],
        scratch_shapes=list(scratch),
        compiler_params=params(mib),
        name=name,
        cost_estimate=pl.CostEstimate(flops=flops, bytes_accessed=10**5, transcendentals=0),
    )


def arr(shape, dtype=F32):
    return jax.ShapeDtypeStruct(shape, dtype)


def registers(x):
    rows = x.size // (SUBS * LANES)
    return x.reshape(rows, 2, 4, LANES).transpose(0, 2, 1, 3).reshape(rows, SUBS, LANES)


def swapped(x, start):
    size = lax.axis_size("tile")
    pairs = [((i + start) % size, (i + start + 1) % size) for i in range(0, size, 2)]
    return lax.ppermute(x, "tile", pairs + [(b, a) for a, b in pairs])


def far(x):
    return pltpu.with_memory_space_constraint(x, HBM)


def shift(x, axis, distance):
    size = lax.axis_size(axis)
    return lax.ppermute(x, axis, [(i, (i + distance) % size) for i in range(size)])


def body(tracer, u_courant, v_courant, surface_flux, mixing, kernel, column, owner_tile, offset, counts):
    c, u, v, f = (registers(x) for x in (tracer, u_courant, v_courant, surface_flux))
    col, own, off = (x.reshape(1, SND) for x in (column, owner_tile, offset))
    block = arr((2 * HERE, SUBS, LANES))
    near_half, far_half, part = call(
        halo_kernel,
        [arr((45, SUBS, LANES)), arr((45, SUBS, LANES)), block],
        [spec(HBM)] * 4,
        [
            pltpu.VMEM((2 * HERE, SUBS, LANES), F32),
            pltpu.VMEM((HERE, SUBS, LANES), F32),
            pltpu.VMEM((HERE, SUBS, LANES), F32),
            pltpu.VMEM((2, SUBS, LANES), F32),
            pltpu.SemaphoreType.DMA((4,)),
        ],
        name="halo",
    )(*(far(x) for x in (c, u, v, f)))
    from_near, from_far = swapped(near_half, 0), swapped(far_half, 1)
    send, place_of, den = call(
        send_kernel,
        [arr((TILES * MESSAGE, LANES)), arr((1, SND), jnp.int32), arr((4, SUBS, LANES))],
        [spec(HBM)] + [spec()] * 4,
        [pltpu.VMEM((HERE, SND), F32), pltpu.VMEM((BOTH, SND), F32), pltpu.VMEM((SUBS, SND), jnp.int32), pltpu.VMEM((SND, WIDE), BF16), pltpu.SemaphoreType.DMA],
        mib=28,
        flops=9 * 10**9,
        name="send",
    )(far(kernel), col, own, off, part)
    adv = call(advect_kernel, arr((40, SUBS, LANES)), [spec()] * 8, name="advect")(
        c, u, v, f, part, from_near, from_far, den
    )
    up, down = shift(adv, "lev", -1), shift(adv, "lev", 1)
    across = [shift(adv, "lev", 2)]
    mark = call(mark_kernel, arr((SUBS, LANES)), [spec()], name="mark")(adv)
    send, mark = lax.optimization_barrier((send, mark))
    got = lax.all_to_all(send.reshape(TILES, 1, MESSAGE * LANES), "tile", 0, 0, tiled=True)
    got = got.reshape(TILES * MESSAGE, LANES)
    transported, field, weight = call(
        mix_kernel,
        [block, arr((SUBS, 2, ROWS, LANES)), arr((4, SUBS, LANES))],
        [spec()] * (5 + len(across)),
        flops=10**11,
        name="mix",
    )(mixing, mark, adv, up, *across, down)
    sums = call(
        sample_kernel,
        arr((3 * TILES, LANES)),
        [spec()] * 2,
        [pltpu.VMEM((8 * FIELD, WIDE), BF16)],
        mib=24,
        name="sample",
    )(got, field)
    back = lax.all_to_all(sums.reshape(TILES, 1, 3 * LANES), "tile", 0, 0, tiled=True)
    back = back.reshape(3 * TILES, LANES)
    mine = call(home_kernel, arr((8, SUBS, LANES)), [spec()] * 2, name="home")(back, place_of)
    nums = [shift(mine, "lev", -d) for d in (1, 2, 3)]
    evolved = call(last_kernel, arr((2, SND)), [spec(SMEM)] + [spec()] * 5, name="last")(counts, mine, *nums, weight)
    out = transported.reshape(2 * HERE, 4, 2, LANES).transpose(0, 2, 1, 3).reshape(tracer.shape)
    return out, evolved


def solution(mesh):
    in_specs = (
        P(None, "lev", "tile", None),
        P("lev", "tile", None),
        P("lev", "tile", None),
        P(None, "tile", None),
        P(),
        P("lev", "tile"),
        P("tile"),
        P("tile"),
        P("tile"),
        P("tile"),
    )
    out_specs = (P(None, "lev", "tile", None), P(None, "tile"))
    return jax.shard_map(body, mesh=mesh, in_specs=in_specs, out_specs=out_specs, check_vma=False)
```

```python
import jax
import jax.numpy as jnp
from jax import lax
from jax.experimental import pallas as pl
from jax.experimental.pallas import tpu as pltpu
from jax.sharding import PartitionSpec as P

LANES = 128
SUBS = 8
HERE = 18
ROWS = 24
TILES = 64
WIDE = 256
QUADS = 8
SND = 4096
F32 = jnp.float32
BF16 = jnp.bfloat16
VMEM = pltpu.MemorySpace.VMEM
SMEM = pltpu.MemorySpace.SMEM
HBM = pltpu.MemorySpace.HBM


def params(mib):
    return pltpu.CompilerParams(vmem_limit_bytes=mib * 2**20)


def spec(space=VMEM):
    return pl.BlockSpec(memory_space=space)


def iota(shape, dim):
    return lax.broadcasted_iota(jnp.int32, shape, dim)


def split(x):
    high = x.astype(BF16)
    low = (x - high.astype(F32)).astype(BF16)
    return high, low


def roll(x, shift, axis):
    return pltpu.roll(x, shift % x.shape[axis], axis)


def swap(x, first):
    return jnp.where(first, roll(x, -1, 0), roll(x, 1, 0))


def inner(c, u, v, first):
    sub, lane = iota(c.shape, 0), iota(c.shape, 1)
    shifted = roll(c, 1, 1)
    south = jnp.where(lane == 0, roll(shifted, 2, 0), shifted)
    wall = (sub < 2) & (lane == 0)
    flux_south = jnp.where(wall, 0.0, v * jnp.where(v > 0, south, c))
    back = roll(flux_south, -1, 1)
    flux_north = jnp.where(lane == LANES - 1, roll(back, -2, 0), back)
    middle = u * jnp.where(u > 0, roll(c, 1, 0), c)
    return c - (flux_north - flux_south) + jnp.where(first, -roll(middle, -1, 0), middle)


def surfaced(c_ref, f_ref, s, level):
    c = c_ref[s * HERE + level]
    if level > 0:
        return c
    return c + jnp.where(lax.axis_index("lev") == 0, f_ref[s], 0.0)


def halo_kernel(c_in, u_in, v_in, f_in, near_ref, far_ref, part_ref, c_ref, u_ref, v_ref, f_ref, sem):
    fetch(((c_in, c_ref), (u_in, u_ref), (v_in, v_ref), (f_in, f_ref)), sem)
    first = iota((SUBS, LANES), 0) % 2 == 0
    even = lax.axis_index("tile") % 2 == 0
    for level in range(HERE):
        u, v = u_ref[level], v_ref[level]
        for s in range(2):
            row = s * HERE + level
            c = surfaced(c_ref, f_ref, s, level)
            y = inner(c, u, v, first)
            part_ref[row] = y
            east = jnp.where(first, roll(c, -1, 0), y)
            west = jnp.where(first, y, roll(c, 1, 0))
            near_ref[row] = jnp.where(even, east, west)
            far_ref[row] = jnp.where(even, west, east)
    for level in range(HERE // 2):
        u = jnp.where(first, u_ref[level], roll(u_ref[level + HERE // 2], 1, 0))
        near_ref[2 * HERE + level] = u
        far_ref[2 * HERE + level] = u


def advect_kernel(c_ref, u_ref, v_ref, f_ref, part_ref, near_ref, far_ref, den_ref, out_ref):
    even = lax.axis_index("tile") % 2 == 0
    first = iota((SUBS, LANES), 0) % 2 == 0
    for level in range(HERE):
        u, v = u_ref[level], v_ref[level]
        row = 2 * HERE + level % (HERE // 2)
        packed = jnp.where(even, near_ref[row], far_ref[row])
        beyond = roll(packed, 1, 0) if level < HERE // 2 else packed
        outer = jnp.where(first, u, beyond)
        forward = outer > 0
        for s in range(2):
            row = s * HERE + level
            c = surfaced(c_ref, f_ref, s, level)
            a = jnp.where(even, far_ref[row], near_ref[row])
            b = jnp.where(even, near_ref[row], far_ref[row])
            flux = outer * jnp.where(forward, jnp.where(first, a, c), jnp.where(first, c, b))
            own = part_ref[row] + jnp.where(first, flux, -flux)
            near = swap(jnp.where(first, b + roll(flux, -1, 0), a - roll(flux, 1, 0)), first)
            flux = outer * jnp.where(forward, jnp.where(first, near, own), jnp.where(first, own, near))
            out_ref[row] = inner(own, u, v, first) + jnp.where(first, flux, -flux)
    for row in range(4):
        out_ref[2 * HERE + row] = den_ref[row]


def mark_kernel(x_ref, out_ref):
    out_ref[...] = x_ref[0]


def mix_kernel(count_ref, mix_ref, mark_ref, *refs):
    *refs, out_ref, field_ref, scale_ref = refs
    size = 2 * HERE + 4

    def block(d, row, count, sub):
        if d == 2 and len(refs) == 5:
            lower, upper = refs[2:4]
            cut = size // 2
            parts = []
            if row < cut:
                parts.append(lower[row : min(row + count, cut), sub, :])
            if row + count > cut:
                parts.append(upper[max(row - cut, 0) : row + count - cut, sub, :])
            return parts[0] if len(parts) == 1 else jnp.concatenate(parts, axis=0)
        return refs[d if d < 3 else -1][row : row + count, sub, :]

    def weights(d, row):
        if d == 2 and len(refs) == 5:
            return refs[3][row - size // 2]
        return refs[d if d < 3 else -1][row]

    z = lax.axis_index("lev")
    level = iota((ROWS, 4 * HERE), 0)
    pick = ((iota((ROWS, 4 * HERE), 1) == z * HERE + level) & (level < HERE)).astype(F32).astype(BF16)
    at = iota((4 * HERE, 4 * ROWS), 1)
    turn = (at >= ROWS).astype(jnp.int32) + (at >= 2 * ROWS).astype(jnp.int32) + (at >= 3 * ROWS).astype(jnp.int32)
    level = at - turn * ROWS
    source = ((z + turn) & 3) * HERE + level
    spread = ((iota((4 * HERE, 4 * ROWS), 0) == source) & (level < HERE)).astype(F32).astype(BF16)

    def chosen(part):
        rows = jnp.dot(pick, part, preferred_element_type=F32).astype(BF16)
        return jnp.dot(rows, spread, preferred_element_type=F32).astype(BF16)

    high, low = (chosen(part) for part in split(mix_ref[...]))
    both = jnp.concatenate([high.astype(F32), low.astype(F32)], axis=0).astype(BF16)
    pad = jnp.zeros((ROWS - HERE, 2 * LANES), F32)
    for s in range(2):
        rows = slice(s * HERE, (s + 1) * HERE)
        for sub in range(0, SUBS, 2):
            parts = []
            for d in range(4):
                parts += [jnp.concatenate([block(d, s * HERE, HERE, sub + i) for i in range(2)], axis=1), pad]
            x_high, x_low = split(jnp.concatenate(parts, axis=0))
            r = jnp.dot(both, x_high, preferred_element_type=F32)
            mixed = r[0:ROWS] + r[ROWS:] + jnp.dot(high, x_low, preferred_element_type=F32)
            for i in range(2):
                half = mixed[:, i * LANES : (i + 1) * LANES]
                field_ref[sub + i, s] = half
                out_ref[rows, sub + i, :] = half[0:HERE]
    for row in range(4):
        a, b, c, d = (weights(i, 2 * HERE + row) for i in range(4))
        number = (row * SUBS + iota((SUBS, LANES), 0)) * LANES + iota((SUBS, LANES), 1)
        scale_ref[row] = jnp.where(number < count_ref[0], 1.0 / ((a + c) + (b + d)), 0.0)


def place(own, rank):
    full = rank < LANES
    group = (own >> 2) * 3 + jnp.where(full, (own & 3) >> 1, 2)
    lane = jnp.where(full, (own & 1) * LANES + rank, (own & 3) * 64 + rank - LANES)
    return group, lane


def fetch(pairs, sem):
    copies = [pltpu.make_async_copy(a, b, sem.at[i]) for i, (a, b) in enumerate(pairs)]
    for copy in copies:
        copy.start()
    for copy in copies:
        copy.wait()


MESSAGE = 29
BOTH = 40


def send_kernel(
    kern_in, col_ref, own_ref, off_ref, part_ref, send_ref, place_ref, den_ref,
    kern_ref, w_ref, grp_ref, hot_ref, sem,
):
    weights = pltpu.make_async_copy(kern_in, kern_ref, sem)
    weights.start()
    before = (iota((WIDE, WIDE), 0) < iota((WIDE, WIDE), 1)).astype(BF16)
    slot = iota((WIDE, 1), 0)
    carry = jnp.zeros((TILES, 1), F32)
    for b in range(SND // WIDE):
        at = pl.ds(b * WIDE, WIDE)
        own = own_ref[:, at]
        onehot = (iota((TILES, WIDE), 0) == own).astype(F32)
        prefix = jnp.dot(onehot.astype(BF16), before, preferred_element_type=F32)
        rank = jnp.sum(onehot * (prefix + carry), axis=0, keepdims=True).astype(jnp.int32)
        carry = carry + jnp.sum(onehot, axis=1, keepdims=True)
        place_ref[:, at] = own * WIDE + rank
        group, lane = place(own, rank)
        grp_ref[:, at] = jnp.broadcast_to(group, (SUBS, WIDE))
        hot_ref[at, :] = (slot == lane).astype(F32).T.astype(BF16)

    weights.wait()
    z = lax.axis_index("lev")
    levels = z * HERE + iota((HERE, SND), 0)
    weighted = jnp.where(levels >= off_ref[...], kern_ref[...], 0.0)
    den = jnp.sum(weighted, axis=0, keepdims=True)
    for j in range(SND // LANES):
        den_ref[j // SUBS, j % SUBS : j % SUBS + 1, :] = den[:, j * LANES : (j + 1) * LANES]
    col = col_ref[...]
    high = weighted.astype(BF16).astype(F32)
    col_high = (col & ~3).astype(F32)
    last = slice(HERE - 2, HERE)
    w_ref[0:16, :] = high[0:16]
    w_ref[16:32, :] = (weighted - high)[0:16]
    w_ref[32:34, :] = high[last]
    w_ref[34:35, :] = col_high
    w_ref[35:37, :] = (weighted - high)[last]
    w_ref[37:38, :] = (col & 3).astype(F32)
    w_ref[38:40, :] = jnp.zeros((2, SND), F32)

    quads, chunk = 16, 512
    sub, left = iota((SUBS, LANES), 0), iota((SUBS, LANES), 1) < 64

    def some(i):
        acc = jnp.zeros((quads * 3 * BOTH, WIDE), F32)
        for b in range(SND // chunk):
            at = pl.ds(b * chunk, chunk)
            w = w_ref[:, at]
            group = grp_ref[:, at]
            rows = []
            for j in range(quads * 3):
                here = group == i * quads * 3 + j
                rows += [jnp.where(here, w[k : k + SUBS], 0.0) for k in range(0, BOTH, SUBS)]
            lhs = jnp.concatenate(rows, axis=0).astype(BF16)
            acc = acc + jnp.dot(lhs, hot_ref[at, :], preferred_element_type=F32)
        for q in range(quads):
            sums = []
            for j in range(3):
                base = (q * 3 + j) * BOTH
                third = acc[base + 32 : base + 40]
                third = third + roll(third, 3 if j == 2 else -3, 0)
                sums.append((acc[base : base + 16] + acc[base + 16 : base + 32], third))
            for k in range(4):
                t = (i * quads + q) * 4 + k
                mine = slice((k % 2) * LANES, (k % 2 + 1) * LANES)
                pair = slice((k // 2) * LANES, (k // 2 + 1) * LANES)
                top, third = (x[:, mine] for x in sums[k // 2])
                rest, middle = (x[:, pair] for x in sums[2])
                if k % 2 == 0:
                    bottom = jnp.where(left, rest[0:8], roll(rest[8:16], 64, 1))
                else:
                    bottom = jnp.where(left, roll(rest[0:8], 64, 1), rest[8:16])
                    middle = roll(middle, 64, 1)
                send_ref[MESSAGE * t : MESSAGE * t + 16, :] = top
                send_ref[MESSAGE * t + 16 : MESSAGE * t + 24, :] = bottom
                after = roll(middle, -1, 0)
                split_row = jnp.where(left, middle, roll(after, 64, 1))
                tail = jnp.where(sub < 3, third, jnp.where(sub == 3, split_row, after))
                send_ref[MESSAGE * t + 24 : MESSAGE * t + 29, :] = tail[0:5]

    for i in range(TILES // (4 * quads)):
        some(i)


FIELD = 40


def sample_kernel(got_ref, field_ref, out_ref, f_ref):
    sub, lane = iota((SUBS, LANES), 0), iota((SUBS, LANES), 1)
    left = lane < 64
    for h in range(4):
        blocks = []
        for lon in range(2):
            x, y = field_ref[2 * h + lon, 0], field_ref[2 * h + lon, 1]
            third = jnp.where(sub < 2, x[16:24], roll(y[16:24], 3, 0))
            blocks.append(jnp.concatenate([x[0:16], y[0:16], third], axis=0))
        high, low = split(jnp.concatenate(blocks, axis=1))
        f_ref[h * FIELD : (h + 1) * FIELD, :] = high
        f_ref[(4 + h) * FIELD : (5 + h) * FIELD, :] = low
    spot = iota((WIDE, 1), 0)
    row = iota((SUBS, WIDE), 0)

    def sums(w, col):
        col = col.astype(jnp.int32)
        hot = (spot == (col & 127) + ((col >> 9) << 7)).astype(F32).astype(BF16)
        block = jnp.broadcast_to((col >> 7) & 3, (SUBS, WIDE))
        hits = [block == h for h in range(4)]
        both = jnp.dot(f_ref[...], hot, preferred_element_type=F32)
        values = both[0 : 4 * FIELD] + both[4 * FIELD :]

        def pick(base):
            out = values[base : base + 8]
            for h in range(1, 4):
                out = jnp.where(hits[h], values[h * FIELD + base : h * FIELD + base + 8], out)
            return out

        last = jnp.where(row < 2, w[2], 0.0)
        last = pick(32) * (last + roll(last, 3, 0))
        totals = []
        for s in range(2):
            total = pick(16 * s) * w[0] + pick(16 * s + 8) * w[1] + jnp.where((row < 3) == (s == 0), last, 0.0)
            totals.append(jnp.sum(total, axis=0, keepdims=True))
        return totals

    def wide(a, b):
        return jnp.concatenate([a, b], axis=1)

    def last_of(x, y):
        a = jnp.where(left, x, roll(y, 64, 1))
        b = jnp.where(left, roll(x, 64, 1), y)
        return jnp.where(sub == 0, roll(a, -3, 0), jnp.where(sub == 1, roll(b, -2, 0), roll(a, -2, 0)))

    quads = QUADS
    half = lane[0:1] < 64

    def some(i, _):
        rows = []
        step = 4 * quads * MESSAGE
        got = got_ref.at[pl.ds(pl.multiple_of(i * step, SUBS), step)]
        for q in range(quads):
            xs = []
            for k in range(4):
                base = (q * 4 + k) * MESSAGE
                tail = jnp.concatenate([got[base + 24 : base + 29, :], jnp.zeros((3, LANES), F32)], axis=0)
                xs.append([got[base : base + 8, :], got[base + 8 : base + 16, :], tail, got[base + 16 : base + 24, :]])
            results, rest = [], []
            for x, y in (xs[0:2], xs[2:4]):
                w = [wide(x[g], y[g]) for g in range(3)]
                results.append(sums(w, w[2][2:3]))
                rest.append(
                    (
                        jnp.where(left, x[3], roll(y[3], 64, 1)),
                        jnp.where(left, roll(x[3], 64, 1), y[3]),
                        last_of(x[2], y[2]),
                    )
                )
            w = [wide(rest[0][g], rest[1][g]) for g in range(3)]
            tails = sums(w, w[2][2:3])
            for k in range(4):
                mine = slice((k % 2) * LANES, (k % 2 + 1) * LANES)
                pair = slice((k // 2) * LANES, (k // 2 + 1) * LANES)
                a, b = tails[0][:, pair], tails[1][:, pair]
                tail = jnp.where(half, a, roll(b, 64, 1)) if k % 2 == 0 else jnp.where(half, roll(a, 64, 1), b)
                rows += [results[k // 2][0][:, mine], results[k // 2][1][:, mine], tail]
        size = 12 * quads
        out_ref[pl.ds(pl.multiple_of(i * size, SUBS), size), :] = jnp.concatenate(rows, axis=0)
        return 0

    lax.fori_loop(0, TILES // (4 * quads), some, 0)


def home_kernel(back_ref, place_ref, out_ref):
    plain, other, tail = (back_ref[pl.ds(j, TILES, stride=3), :] for j in range(3))
    first = jnp.concatenate([plain, tail], axis=1)
    second = jnp.concatenate([other, roll(tail, 64, 1)], axis=1)
    parts = jnp.concatenate(split(jnp.concatenate([first, second], axis=0)), axis=0)
    slot = iota((WIDE, 1), 0)
    for b in range(SND // WIDE):
        at = pl.ds(b * WIDE, WIDE)
        hot = (slot == (place_ref[:, at] & (WIDE - 1))).astype(F32).astype(BF16)
        both = jnp.dot(parts, hot, preferred_element_type=F32)
        values = both[0 : 2 * TILES] + both[2 * TILES :]
        mine = iota((TILES, WIDE), 0) == (place_ref[:, at] >> 8)
        for s in range(2):
            picked = jnp.where(mine, values[s * TILES : (s + 1) * TILES], 0.0)
            total = jnp.sum(picked, axis=0, keepdims=True)
            for i in range(2):
                j = s * 32 + 2 * b + i
                out_ref[j // SUBS, j % SUBS : j % SUBS + 1, :] = total[:, i * LANES : (i + 1) * LANES]


def last_kernel(a_ref, b_ref, d_ref, c_ref, scale_ref, out_ref):
    for row in range(4):
        scale = scale_ref[row]
        for s in range(2):
            k = s * 4 + row
            num = (a_ref[k] + c_ref[k]) + (b_ref[k] + d_ref[k])
            value = jnp.where(scale > 0, num * scale, 0.0)
            for j in range(SUBS):
                at = (row * SUBS + j) * LANES
                out_ref[s : s + 1, at : at + LANES] = value[j : j + 1]


def call(kernel, outs, in_specs, scratch=(), mib=12, flops=10**6, name=None):
    single = not isinstance(outs, (list, tuple))
    shapes = [outs] if single else outs
    return pl.pallas_call(
        kernel,
        out_shape=outs if single else list(outs),
        in_specs=in_specs,
        out_specs=spec() if single else [spec() for _ in shapes],
        scratch_shapes=list(scratch),
        compiler_params=params(mib),
        name=name,
        cost_estimate=pl.CostEstimate(flops=flops, bytes_accessed=10**5, transcendentals=0),
    )


def arr(shape, dtype=F32):
    return jax.ShapeDtypeStruct(shape, dtype)


def registers(x):
    rows = x.size // (SUBS * LANES)
    return x.reshape(rows, 2, 4, LANES).transpose(0, 2, 1, 3).reshape(rows, SUBS, LANES)


def swapped(x, start):
    size = lax.axis_size("tile")
    pairs = [((i + start) % size, (i + start + 1) % size) for i in range(0, size, 2)]
    return lax.ppermute(x, "tile", pairs + [(b, a) for a, b in pairs])


def far(x):
    return pltpu.with_memory_space_constraint(x, HBM)


def shift(x, axis, distance):
    size = lax.axis_size(axis)
    return lax.ppermute(x, axis, [(i, (i + distance) % size) for i in range(size)])


def body(tracer, u_courant, v_courant, surface_flux, mixing, kernel, column, owner_tile, offset, counts):
    c, u, v, f = (registers(x) for x in (tracer, u_courant, v_courant, surface_flux))
    col, own, off = (x.reshape(1, SND) for x in (column, owner_tile, offset))
    block = arr((2 * HERE, SUBS, LANES))
    near_half, far_half, part = call(
        halo_kernel,
        [arr((45, SUBS, LANES)), arr((45, SUBS, LANES)), block],
        [spec(HBM)] * 4,
        [
            pltpu.VMEM((2 * HERE, SUBS, LANES), F32),
            pltpu.VMEM((HERE, SUBS, LANES), F32),
            pltpu.VMEM((HERE, SUBS, LANES), F32),
            pltpu.VMEM((2, SUBS, LANES), F32),
            pltpu.SemaphoreType.DMA((4,)),
        ],
        name="halo",
    )(*(far(x) for x in (c, u, v, f)))
    from_near, from_far = swapped(near_half, 0), swapped(far_half, 1)
    send, place_of, den = call(
        send_kernel,
        [arr((TILES * MESSAGE, LANES)), arr((1, SND), jnp.int32), arr((4, SUBS, LANES))],
        [spec(HBM)] + [spec()] * 4,
        [pltpu.VMEM((HERE, SND), F32), pltpu.VMEM((BOTH, SND), F32), pltpu.VMEM((SUBS, SND), jnp.int32), pltpu.VMEM((SND, WIDE), BF16), pltpu.SemaphoreType.DMA],
        mib=28,
        flops=9 * 10**9,
        name="send",
    )(far(kernel), col, own, off, part)
    adv = call(advect_kernel, arr((40, SUBS, LANES)), [spec()] * 8, name="advect")(
        c, u, v, f, part, from_near, from_far, den
    )
    up, down = shift(adv, "lev", -1), shift(adv, "lev", 1)
    across = [shift(adv, "lev", 2)]
    mark = call(mark_kernel, arr((SUBS, LANES)), [spec()], name="mark")(adv)
    send, mark = lax.optimization_barrier((send, mark))
    got = lax.all_to_all(send.reshape(TILES, 1, MESSAGE * LANES), "tile", 0, 0, tiled=True)
    got = got.reshape(TILES * MESSAGE, LANES)
    transported, field, scale = call(
        mix_kernel,
        [block, arr((SUBS, 2, ROWS, LANES)), arr((4, SUBS, LANES))],
        [spec(SMEM)] + [spec()] * (5 + len(across)),
        flops=10**11,
        name="mix",
    )(counts, mixing, mark, adv, up, *across, down)
    sums = call(
        sample_kernel,
        arr((3 * TILES, LANES)),
        [spec()] * 2,
        [pltpu.VMEM((8 * FIELD, WIDE), BF16)],
        mib=24,
        name="sample",
    )(got, field)
    back = lax.all_to_all(sums.reshape(TILES, 1, 3 * LANES), "tile", 0, 0, tiled=True)
    back = back.reshape(3 * TILES, LANES)
    mine = call(home_kernel, arr((8, SUBS, LANES)), [spec()] * 2, name="home")(back, place_of)
    nums = [shift(mine, "lev", -d) for d in (1, 2, 3)]
    evolved = call(last_kernel, arr((2, SND)), [spec()] * 5, name="last")(mine, nums[0], nums[2], nums[1], scale)
    out = transported.reshape(2 * HERE, 4, 2, LANES).transpose(0, 2, 1, 3).reshape(tracer.shape)
    return out, evolved


def solution(mesh):
    in_specs = (
        P(None, "lev", "tile", None),
        P("lev", "tile", None),
        P("lev", "tile", None),
        P(None, "tile", None),
        P(),
        P("lev", "tile"),
        P("tile"),
        P("tile"),
        P("tile"),
        P("tile"),
    )
    out_specs = (P(None, "lev", "tile", None), P(None, "tile"))
    return jax.shard_map(body, mesh=mesh, in_specs=in_specs, out_specs=out_specs, check_vma=False)
```

```python
import jax
import jax.numpy as jnp
from jax import lax
from jax.experimental import pallas as pl
from jax.experimental.pallas import tpu as pltpu
from jax.sharding import PartitionSpec as P

LANES = 128
SUBS = 8
HERE = 18
ROWS = 24
TILES = 64
WIDE = 256
QUADS = 8
SND = 4096
F32 = jnp.float32
BF16 = jnp.bfloat16
VMEM = pltpu.MemorySpace.VMEM
SMEM = pltpu.MemorySpace.SMEM
HBM = pltpu.MemorySpace.HBM


def params(mib):
    return pltpu.CompilerParams(vmem_limit_bytes=mib * 2**20)


def spec(space=VMEM):
    return pl.BlockSpec(memory_space=space)


def iota(shape, dim):
    return lax.broadcasted_iota(jnp.int32, shape, dim)


def split(x):
    high = x.astype(BF16)
    low = (x - high.astype(F32)).astype(BF16)
    return high, low


def roll(x, shift, axis):
    return pltpu.roll(x, shift % x.shape[axis], axis)


def swap(x, first):
    return jnp.where(first, roll(x, -1, 0), roll(x, 1, 0))


def inner(c, u, v, first):
    sub, lane = iota(c.shape, 0), iota(c.shape, 1)
    shifted = roll(c, 1, 1)
    south = jnp.where(lane == 0, roll(shifted, 2, 0), shifted)
    wall = (sub < 2) & (lane == 0)
    flux_south = jnp.where(wall, 0.0, v * jnp.where(v > 0, south, c))
    back = roll(flux_south, -1, 1)
    flux_north = jnp.where(lane == LANES - 1, roll(back, -2, 0), back)
    middle = u * jnp.where(u > 0, roll(c, 1, 0), c)
    return c - (flux_north - flux_south) + jnp.where(first, -roll(middle, -1, 0), middle)


def surfaced(c_ref, f_ref, s, level):
    c = c_ref[s * HERE + level]
    if level > 0:
        return c
    return c + jnp.where(lax.axis_index("lev") == 0, f_ref[s], 0.0)


def halo_kernel(c_in, u_in, v_in, f_in, near_ref, far_ref, part_ref, c_ref, u_ref, v_ref, f_ref, sem):
    fetch(((c_in, c_ref), (u_in, u_ref), (v_in, v_ref), (f_in, f_ref)), sem)
    first = iota((SUBS, LANES), 0) % 2 == 0
    even = lax.axis_index("tile") % 2 == 0
    for level in range(HERE):
        u, v = u_ref[level], v_ref[level]
        for s in range(2):
            row = s * HERE + level
            c = surfaced(c_ref, f_ref, s, level)
            y = inner(c, u, v, first)
            part_ref[row] = y
            east = jnp.where(first, roll(c, -1, 0), y)
            west = jnp.where(first, y, roll(c, 1, 0))
            near_ref[row] = jnp.where(even, east, west)
            far_ref[row] = jnp.where(even, west, east)
    for level in range(HERE // 2):
        u = jnp.where(first, u_ref[level], roll(u_ref[level + HERE // 2], 1, 0))
        near_ref[2 * HERE + level] = u
        far_ref[2 * HERE + level] = u


def advect_kernel(c_ref, u_ref, v_ref, f_ref, part_ref, near_ref, far_ref, den_ref, out_ref):
    even = lax.axis_index("tile") % 2 == 0
    first = iota((SUBS, LANES), 0) % 2 == 0
    for level in range(HERE):
        u, v = u_ref[level], v_ref[level]
        row = 2 * HERE + level % (HERE // 2)
        packed = jnp.where(even, near_ref[row], far_ref[row])
        beyond = roll(packed, 1, 0) if level < HERE // 2 else packed
        outer = jnp.where(first, u, beyond)
        forward = outer > 0
        for s in range(2):
            row = s * HERE + level
            c = surfaced(c_ref, f_ref, s, level)
            a = jnp.where(even, far_ref[row], near_ref[row])
            b = jnp.where(even, near_ref[row], far_ref[row])
            flux = outer * jnp.where(forward, jnp.where(first, a, c), jnp.where(first, c, b))
            own = part_ref[row] + jnp.where(first, flux, -flux)
            near = swap(jnp.where(first, b + roll(flux, -1, 0), a - roll(flux, 1, 0)), first)
            flux = outer * jnp.where(forward, jnp.where(first, near, own), jnp.where(first, own, near))
            out_ref[row] = inner(own, u, v, first) + jnp.where(first, flux, -flux)
    for row in range(4):
        out_ref[2 * HERE + row] = den_ref[row]


def mark_kernel(x_ref, out_ref):
    out_ref[...] = x_ref[0]


def mix_kernel(count_ref, mix_ref, mark_ref, *refs):
    *refs, out_ref, field_ref, scale_ref = refs
    refs = [refs[i] for i in (0, 1, 3, 2)]
    size = 2 * HERE + 4

    def block(d, row, count, sub):
        if d == 2 and len(refs) == 5:
            lower, upper = refs[2:4]
            cut = size // 2
            parts = []
            if row < cut:
                parts.append(lower[row : min(row + count, cut), sub, :])
            if row + count > cut:
                parts.append(upper[max(row - cut, 0) : row + count - cut, sub, :])
            return parts[0] if len(parts) == 1 else jnp.concatenate(parts, axis=0)
        return refs[d if d < 3 else -1][row : row + count, sub, :]

    def weights(d, row):
        if d == 2 and len(refs) == 5:
            return refs[3][row - size // 2]
        return refs[d if d < 3 else -1][row]

    z = lax.axis_index("lev")
    level = iota((ROWS, 4 * HERE), 0)
    pick = ((iota((ROWS, 4 * HERE), 1) == z * HERE + level) & (level < HERE)).astype(F32).astype(BF16)
    at = iota((4 * HERE, 4 * ROWS), 1)
    turn = (at >= ROWS).astype(jnp.int32) + (at >= 2 * ROWS).astype(jnp.int32) + (at >= 3 * ROWS).astype(jnp.int32)
    level = at - turn * ROWS
    source = ((z + turn) & 3) * HERE + level
    spread = ((iota((4 * HERE, 4 * ROWS), 0) == source) & (level < HERE)).astype(F32).astype(BF16)

    def chosen(part):
        rows = jnp.dot(pick, part, preferred_element_type=F32).astype(BF16)
        return jnp.dot(rows, spread, preferred_element_type=F32).astype(BF16)

    high, low = (chosen(part) for part in split(mix_ref[...]))
    both = jnp.concatenate([high.astype(F32), low.astype(F32)], axis=0).astype(BF16)
    pad = jnp.zeros((ROWS - HERE, 2 * LANES), F32)
    for s in range(2):
        rows = slice(s * HERE, (s + 1) * HERE)
        for sub in range(0, SUBS, 2):
            parts = []
            for d in range(4):
                parts += [jnp.concatenate([block(d, s * HERE, HERE, sub + i) for i in range(2)], axis=1), pad]
            x_high, x_low = split(jnp.concatenate(parts, axis=0))
            r = jnp.dot(both, x_high, preferred_element_type=F32)
            mixed = r[0:ROWS] + r[ROWS:] + jnp.dot(high, x_low, preferred_element_type=F32)
            for i in range(2):
                half = mixed[:, i * LANES : (i + 1) * LANES]
                field_ref[sub + i, s] = half
                out_ref[rows, sub + i, :] = half[0:HERE]
    for row in range(4):
        a, b, c, d = (weights(i, 2 * HERE + row) for i in range(4))
        number = (row * SUBS + iota((SUBS, LANES), 0)) * LANES + iota((SUBS, LANES), 1)
        scale_ref[row] = jnp.where(number < count_ref[0], 1.0 / ((a + c) + (b + d)), 0.0)


def place(own, rank):
    full = rank < LANES
    group = (own >> 2) * 3 + jnp.where(full, (own & 3) >> 1, 2)
    lane = jnp.where(full, (own & 1) * LANES + rank, (own & 3) * 64 + rank - LANES)
    return group, lane


def fetch(pairs, sem):
    copies = [pltpu.make_async_copy(a, b, sem.at[i]) for i, (a, b) in enumerate(pairs)]
    for copy in copies:
        copy.start()
    for copy in copies:
        copy.wait()


MESSAGE = 29
BOTH = 40


def send_kernel(
    kern_in, col_ref, own_ref, off_ref, part_ref, send_ref, place_ref, den_ref,
    kern_ref, w_ref, grp_ref, hot_ref, sem,
):
    weights = pltpu.make_async_copy(kern_in, kern_ref, sem)
    weights.start()
    before = (iota((WIDE, WIDE), 0) < iota((WIDE, WIDE), 1)).astype(BF16)
    slot = iota((WIDE, 1), 0)
    carry = jnp.zeros((TILES, 1), F32)
    for b in range(SND // WIDE):
        at = pl.ds(b * WIDE, WIDE)
        own = own_ref[:, at]
        onehot = (iota((TILES, WIDE), 0) == own).astype(F32)
        prefix = jnp.dot(onehot.astype(BF16), before, preferred_element_type=F32)
        rank = jnp.sum(onehot * (prefix + carry), axis=0, keepdims=True).astype(jnp.int32)
        carry = carry + jnp.sum(onehot, axis=1, keepdims=True)
        place_ref[:, at] = own * WIDE + rank
        group, lane = place(own, rank)
        grp_ref[:, at] = jnp.broadcast_to(group, (SUBS, WIDE))
        hot_ref[at, :] = (slot == lane).astype(F32).T.astype(BF16)

    weights.wait()
    z = lax.axis_index("lev")
    levels = z * HERE + iota((HERE, SND), 0)
    weighted = jnp.where(levels >= off_ref[...], kern_ref[...], 0.0)
    den = jnp.sum(weighted, axis=0, keepdims=True)
    for j in range(SND // LANES):
        den_ref[j // SUBS, j % SUBS : j % SUBS + 1, :] = den[:, j * LANES : (j + 1) * LANES]
    col = col_ref[...]
    high = weighted.astype(BF16).astype(F32)
    col_high = (col & ~3).astype(F32)
    last = slice(HERE - 2, HERE)
    w_ref[0:16, :] = high[0:16]
    w_ref[16:32, :] = (weighted - high)[0:16]
    w_ref[32:34, :] = high[last]
    w_ref[34:35, :] = col_high
    w_ref[35:37, :] = (weighted - high)[last]
    w_ref[37:38, :] = (col & 3).astype(F32)
    w_ref[38:40, :] = jnp.zeros((2, SND), F32)

    quads, chunk = 16, 512
    sub, left = iota((SUBS, LANES), 0), iota((SUBS, LANES), 1) < 64

    def some(i):
        acc = jnp.zeros((quads * 3 * BOTH, WIDE), F32)
        for b in range(SND // chunk):
            at = pl.ds(b * chunk, chunk)
            w = w_ref[:, at]
            group = grp_ref[:, at]
            rows = []
            for j in range(quads * 3):
                here = group == i * quads * 3 + j
                rows += [jnp.where(here, w[k : k + SUBS], 0.0) for k in range(0, BOTH, SUBS)]
            lhs = jnp.concatenate(rows, axis=0).astype(BF16)
            acc = acc + jnp.dot(lhs, hot_ref[at, :], preferred_element_type=F32)
        for q in range(quads):
            sums = []
            for j in range(3):
                base = (q * 3 + j) * BOTH
                third = acc[base + 32 : base + 40]
                third = third + roll(third, 3 if j == 2 else -3, 0)
                sums.append((acc[base : base + 16] + acc[base + 16 : base + 32], third))
            for k in range(4):
                t = (i * quads + q) * 4 + k
                mine = slice((k % 2) * LANES, (k % 2 + 1) * LANES)
                pair = slice((k // 2) * LANES, (k // 2 + 1) * LANES)
                top, third = (x[:, mine] for x in sums[k // 2])
                rest, middle = (x[:, pair] for x in sums[2])
                if k % 2 == 0:
                    bottom = jnp.where(left, rest[0:8], roll(rest[8:16], 64, 1))
                else:
                    bottom = jnp.where(left, roll(rest[0:8], 64, 1), rest[8:16])
                    middle = roll(middle, 64, 1)
                send_ref[MESSAGE * t : MESSAGE * t + 16, :] = top
                send_ref[MESSAGE * t + 16 : MESSAGE * t + 24, :] = bottom
                after = roll(middle, -1, 0)
                split_row = jnp.where(left, middle, roll(after, 64, 1))
                tail = jnp.where(sub < 3, third, jnp.where(sub == 3, split_row, after))
                send_ref[MESSAGE * t + 24 : MESSAGE * t + 29, :] = tail[0:5]

    for i in range(TILES // (4 * quads)):
        some(i)


FIELD = 40


def sample_kernel(got_ref, field_ref, out_ref, f_ref):
    sub, lane = iota((SUBS, LANES), 0), iota((SUBS, LANES), 1)
    left = lane < 64
    for h in range(4):
        blocks = []
        for lon in range(2):
            x, y = field_ref[2 * h + lon, 0], field_ref[2 * h + lon, 1]
            third = jnp.where(sub < 2, x[16:24], roll(y[16:24], 3, 0))
            blocks.append(jnp.concatenate([x[0:16], y[0:16], third], axis=0))
        high, low = split(jnp.concatenate(blocks, axis=1))
        f_ref[h * FIELD : (h + 1) * FIELD, :] = high
        f_ref[(4 + h) * FIELD : (5 + h) * FIELD, :] = low
    spot = iota((WIDE, 1), 0)
    row = iota((SUBS, WIDE), 0)

    def sums(w, col):
        col = col.astype(jnp.int32)
        hot = (spot == (col & 127) + ((col >> 9) << 7)).astype(F32).astype(BF16)
        block = jnp.broadcast_to((col >> 7) & 3, (SUBS, WIDE))
        hits = [block == h for h in range(4)]
        both = jnp.dot(f_ref[...], hot, preferred_element_type=F32)
        values = both[0 : 4 * FIELD] + both[4 * FIELD :]

        def pick(base):
            out = values[base : base + 8]
            for h in range(1, 4):
                out = jnp.where(hits[h], values[h * FIELD + base : h * FIELD + base + 8], out)
            return out

        last = jnp.where(row < 2, w[2], 0.0)
        last = pick(32) * (last + roll(last, 3, 0))
        totals = []
        for s in range(2):
            total = pick(16 * s) * w[0] + pick(16 * s + 8) * w[1] + jnp.where((row < 3) == (s == 0), last, 0.0)
            totals.append(jnp.sum(total, axis=0, keepdims=True))
        return totals

    def wide(a, b):
        return jnp.concatenate([a, b], axis=1)

    def last_of(x, y):
        a = jnp.where(left, x, roll(y, 64, 1))
        b = jnp.where(left, roll(x, 64, 1), y)
        return jnp.where(sub == 0, roll(a, -3, 0), jnp.where(sub == 1, roll(b, -2, 0), roll(a, -2, 0)))

    quads = QUADS
    half = lane[0:1] < 64

    def some(i, _):
        rows = []
        step = 4 * quads * MESSAGE
        got = got_ref.at[pl.ds(pl.multiple_of(i * step, SUBS), step)]
        for q in range(quads):
            xs = []
            for k in range(4):
                base = (q * 4 + k) * MESSAGE
                tail = jnp.concatenate([got[base + 24 : base + 29, :], jnp.zeros((3, LANES), F32)], axis=0)
                xs.append([got[base : base + 8, :], got[base + 8 : base + 16, :], tail, got[base + 16 : base + 24, :]])
            results, rest = [], []
            for x, y in (xs[0:2], xs[2:4]):
                w = [wide(x[g], y[g]) for g in range(3)]
                results.append(sums(w, w[2][2:3]))
                rest.append(
                    (
                        jnp.where(left, x[3], roll(y[3], 64, 1)),
                        jnp.where(left, roll(x[3], 64, 1), y[3]),
                        last_of(x[2], y[2]),
                    )
                )
            w = [wide(rest[0][g], rest[1][g]) for g in range(3)]
            tails = sums(w, w[2][2:3])
            for k in range(4):
                mine = slice((k % 2) * LANES, (k % 2 + 1) * LANES)
                pair = slice((k // 2) * LANES, (k // 2 + 1) * LANES)
                a, b = tails[0][:, pair], tails[1][:, pair]
                tail = jnp.where(half, a, roll(b, 64, 1)) if k % 2 == 0 else jnp.where(half, roll(a, 64, 1), b)
                rows += [results[k // 2][0][:, mine], results[k // 2][1][:, mine], tail]
        size = 12 * quads
        out_ref[pl.ds(pl.multiple_of(i * size, SUBS), size), :] = jnp.concatenate(rows, axis=0)
        return 0

    lax.fori_loop(0, TILES // (4 * quads), some, 0)


def home_kernel(back_ref, place_ref, out_ref):
    plain, other, tail = (back_ref[pl.ds(j, TILES, stride=3), :] for j in range(3))
    first = jnp.concatenate([plain, tail], axis=1)
    second = jnp.concatenate([other, roll(tail, 64, 1)], axis=1)
    parts = jnp.concatenate(split(jnp.concatenate([first, second], axis=0)), axis=0)
    slot = iota((WIDE, 1), 0)
    for b in range(SND // WIDE):
        at = pl.ds(b * WIDE, WIDE)
        hot = (slot == (place_ref[:, at] & (WIDE - 1))).astype(F32).astype(BF16)
        both = jnp.dot(parts, hot, preferred_element_type=F32)
        values = both[0 : 2 * TILES] + both[2 * TILES :]
        mine = iota((TILES, WIDE), 0) == (place_ref[:, at] >> 8)
        for s in range(2):
            picked = jnp.where(mine, values[s * TILES : (s + 1) * TILES], 0.0)
            total = jnp.sum(picked, axis=0, keepdims=True)
            for i in range(2):
                j = s * 32 + 2 * b + i
                out_ref[j // SUBS, j % SUBS : j % SUBS + 1, :] = total[:, i * LANES : (i + 1) * LANES]


def last_kernel(a_ref, b_ref, d_ref, c_ref, scale_ref, out_ref):
    for row in range(4):
        scale = scale_ref[row]
        for s in range(2):
            k = s * 4 + row
            num = (a_ref[k] + c_ref[k]) + (b_ref[k] + d_ref[k])
            value = jnp.where(scale > 0, num * scale, 0.0)
            for j in range(SUBS):
                at = (row * SUBS + j) * LANES
                out_ref[s : s + 1, at : at + LANES] = value[j : j + 1]


def call(kernel, outs, in_specs, scratch=(), mib=12, flops=10**6, name=None):
    single = not isinstance(outs, (list, tuple))
    shapes = [outs] if single else outs
    return pl.pallas_call(
        kernel,
        out_shape=outs if single else list(outs),
        in_specs=in_specs,
        out_specs=spec() if single else [spec() for _ in shapes],
        scratch_shapes=list(scratch),
        compiler_params=params(mib),
        name=name,
        cost_estimate=pl.CostEstimate(flops=flops, bytes_accessed=10**5, transcendentals=0),
    )


def arr(shape, dtype=F32):
    return jax.ShapeDtypeStruct(shape, dtype)


def registers(x):
    rows = x.size // (SUBS * LANES)
    return x.reshape(rows, 2, 4, LANES).transpose(0, 2, 1, 3).reshape(rows, SUBS, LANES)


def swapped(x, start):
    size = lax.axis_size("tile")
    pairs = [((i + start) % size, (i + start + 1) % size) for i in range(0, size, 2)]
    return lax.ppermute(x, "tile", pairs + [(b, a) for a, b in pairs])


def far(x):
    return pltpu.with_memory_space_constraint(x, HBM)


def shift(x, axis, distance):
    size = lax.axis_size(axis)
    return lax.ppermute(x, axis, [(i, (i + distance) % size) for i in range(size)])


def body(tracer, u_courant, v_courant, surface_flux, mixing, kernel, column, owner_tile, offset, counts):
    c, u, v, f = (registers(x) for x in (tracer, u_courant, v_courant, surface_flux))
    col, own, off = (x.reshape(1, SND) for x in (column, owner_tile, offset))
    block = arr((2 * HERE, SUBS, LANES))
    near_half, far_half, part = call(
        halo_kernel,
        [arr((45, SUBS, LANES)), arr((45, SUBS, LANES)), block],
        [spec(HBM)] * 4,
        [
            pltpu.VMEM((2 * HERE, SUBS, LANES), F32),
            pltpu.VMEM((HERE, SUBS, LANES), F32),
            pltpu.VMEM((HERE, SUBS, LANES), F32),
            pltpu.VMEM((2, SUBS, LANES), F32),
            pltpu.SemaphoreType.DMA((4,)),
        ],
        name="halo",
    )(*(far(x) for x in (c, u, v, f)))
    from_near, from_far = swapped(near_half, 0), swapped(far_half, 1)
    send, place_of, den = call(
        send_kernel,
        [arr((TILES * MESSAGE, LANES)), arr((1, SND), jnp.int32), arr((4, SUBS, LANES))],
        [spec(HBM)] + [spec()] * 4,
        [pltpu.VMEM((HERE, SND), F32), pltpu.VMEM((BOTH, SND), F32), pltpu.VMEM((SUBS, SND), jnp.int32), pltpu.VMEM((SND, WIDE), BF16), pltpu.SemaphoreType.DMA],
        mib=28,
        flops=9 * 10**9,
        name="send",
    )(far(kernel), col, own, off, part)
    adv = call(advect_kernel, arr((40, SUBS, LANES)), [spec()] * 8, name="advect")(
        c, u, v, f, part, from_near, from_far, den
    )
    up, down = shift(adv, "lev", -1), shift(adv, "lev", 1)
    across = [shift(adv, "lev", 2)]
    mark = call(mark_kernel, arr((SUBS, LANES)), [spec()], name="mark")(adv)
    send, mark = lax.optimization_barrier((send, mark))
    got = lax.all_to_all(send.reshape(TILES, 1, MESSAGE * LANES), "tile", 0, 0, tiled=True)
    got = got.reshape(TILES * MESSAGE, LANES)
    transported, field, scale = call(
        mix_kernel,
        [block, arr((SUBS, 2, ROWS, LANES)), arr((4, SUBS, LANES))],
        [spec(SMEM)] + [spec()] * (5 + len(across)),
        flops=10**11,
        name="mix",
    )(counts, mixing, mark, adv, up, down, *across)
    sums = call(
        sample_kernel,
        arr((3 * TILES, LANES)),
        [spec()] * 2,
        [pltpu.VMEM((8 * FIELD, WIDE), BF16)],
        mib=24,
        name="sample",
    )(got, field)
    back = lax.all_to_all(sums.reshape(TILES, 1, 3 * LANES), "tile", 0, 0, tiled=True)
    back = back.reshape(3 * TILES, LANES)
    mine = call(home_kernel, arr((8, SUBS, LANES)), [spec()] * 2, name="home")(back, place_of)
    nums = [shift(mine, "lev", -d) for d in (1, 2, 3)]
    evolved = call(last_kernel, arr((2, SND)), [spec()] * 5, name="last")(mine, nums[0], nums[2], nums[1], scale)
    out = transported.reshape(2 * HERE, 4, 2, LANES).transpose(0, 2, 1, 3).reshape(tracer.shape)
    return out, evolved


def solution(mesh):
    in_specs = (
        P(None, "lev", "tile", None),
        P("lev", "tile", None),
        P("lev", "tile", None),
        P(None, "tile", None),
        P(),
        P("lev", "tile"),
        P("tile"),
        P("tile"),
        P("tile"),
        P("tile"),
    )
    out_specs = (P(None, "lev", "tile", None), P(None, "tile"))
    return jax.shard_map(body, mesh=mesh, in_specs=in_specs, out_specs=out_specs, check_vma=False)
```

```python
import jax
import jax.numpy as jnp
from jax import lax
from jax.experimental import pallas as pl
from jax.experimental.pallas import tpu as pltpu
from jax.sharding import PartitionSpec as P

LANES = 128
SUBS = 8
HERE = 18
ROWS = 24
TILES = 64
WIDE = 256
QUADS = 8
SND = 4096
F32 = jnp.float32
BF16 = jnp.bfloat16
VMEM = pltpu.MemorySpace.VMEM
SMEM = pltpu.MemorySpace.SMEM
HBM = pltpu.MemorySpace.HBM


def params(mib):
    return pltpu.CompilerParams(vmem_limit_bytes=mib * 2**20)


def spec(space=VMEM):
    return pl.BlockSpec(memory_space=space)


def iota(shape, dim):
    return lax.broadcasted_iota(jnp.int32, shape, dim)


def split(x):
    high = x.astype(BF16)
    low = (x - high.astype(F32)).astype(BF16)
    return high, low


def roll(x, shift, axis):
    return pltpu.roll(x, shift % x.shape[axis], axis)


def swap(x, first):
    return jnp.where(first, roll(x, -1, 0), roll(x, 1, 0))


def inner(c, u, v, first):
    sub, lane = iota(c.shape, 0), iota(c.shape, 1)
    shifted = roll(c, 1, 1)
    south = jnp.where(lane == 0, roll(shifted, 2, 0), shifted)
    wall = (sub < 2) & (lane == 0)
    flux_south = jnp.where(wall, 0.0, v * jnp.where(v > 0, south, c))
    back = roll(flux_south, -1, 1)
    flux_north = jnp.where(lane == LANES - 1, roll(back, -2, 0), back)
    middle = u * jnp.where(u > 0, roll(c, 1, 0), c)
    return c - (flux_north - flux_south) + jnp.where(first, -roll(middle, -1, 0), middle)


def surfaced(c_ref, f_ref, s, level):
    c = c_ref[s * HERE + level]
    if level > 0:
        return c
    return c + jnp.where(lax.axis_index("lev") == 0, f_ref[s], 0.0)


def halo_kernel(c_in, u_in, v_in, f_in, near_ref, far_ref, part_ref, c_ref, u_ref, v_ref, f_ref, sem):
    fetch(((c_in, c_ref), (u_in, u_ref), (v_in, v_ref), (f_in, f_ref)), sem)
    first = iota((SUBS, LANES), 0) % 2 == 0
    even = lax.axis_index("tile") % 2 == 0
    for level in range(HERE):
        u, v = u_ref[level], v_ref[level]
        for s in range(2):
            row = s * HERE + level
            c = surfaced(c_ref, f_ref, s, level)
            y = inner(c, u, v, first)
            part_ref[row] = y
            east = jnp.where(first, roll(c, -1, 0), y)
            west = jnp.where(first, y, roll(c, 1, 0))
            near_ref[row] = jnp.where(even, east, west)
            far_ref[row] = jnp.where(even, west, east)
    for level in range(HERE // 2):
        u = jnp.where(first, u_ref[level], roll(u_ref[level + HERE // 2], 1, 0))
        near_ref[2 * HERE + level] = u
        far_ref[2 * HERE + level] = u


def advect_kernel(c_ref, u_ref, v_ref, f_ref, part_ref, near_ref, far_ref, den_ref, out_ref):
    even = lax.axis_index("tile") % 2 == 0
    first = iota((SUBS, LANES), 0) % 2 == 0
    for level in range(HERE):
        u, v = u_ref[level], v_ref[level]
        row = 2 * HERE + level % (HERE // 2)
        packed = jnp.where(even, near_ref[row], far_ref[row])
        beyond = roll(packed, 1, 0) if level < HERE // 2 else packed
        outer = jnp.where(first, u, beyond)
        forward = outer > 0
        for s in range(2):
            row = s * HERE + level
            c = surfaced(c_ref, f_ref, s, level)
            a = jnp.where(even, far_ref[row], near_ref[row])
            b = jnp.where(even, near_ref[row], far_ref[row])
            flux = outer * jnp.where(forward, jnp.where(first, a, c), jnp.where(first, c, b))
            own = part_ref[row] + jnp.where(first, flux, -flux)
            near = swap(jnp.where(first, b + roll(flux, -1, 0), a - roll(flux, 1, 0)), first)
            flux = outer * jnp.where(forward, jnp.where(first, near, own), jnp.where(first, own, near))
            out_ref[row] = inner(own, u, v, first) + jnp.where(first, flux, -flux)
    for row in range(4):
        out_ref[2 * HERE + row] = den_ref[row]


def mark_kernel(x_ref, out_ref):
    out_ref[...] = x_ref[0]


def mix_kernel(count_ref, mix_ref, mark_ref, *refs):
    *refs, out_ref, field_ref, scale_ref = refs
    refs = [refs[i] for i in (0, 1, 3, 2)]
    size = 2 * HERE + 4

    def block(d, row, count, sub):
        if d == 2 and len(refs) == 5:
            lower, upper = refs[2:4]
            cut = size // 2
            parts = []
            if row < cut:
                parts.append(lower[row : min(row + count, cut), sub, :])
            if row + count > cut:
                parts.append(upper[max(row - cut, 0) : row + count - cut, sub, :])
            return parts[0] if len(parts) == 1 else jnp.concatenate(parts, axis=0)
        return refs[d if d < 3 else -1][row : row + count, sub, :]

    def weights(d, row):
        if d == 2 and len(refs) == 5:
            return refs[3][row - size // 2]
        return refs[d if d < 3 else -1][row]

    z = lax.axis_index("lev")
    level = iota((ROWS, 4 * HERE), 0)
    pick = ((iota((ROWS, 4 * HERE), 1) == z * HERE + level) & (level < HERE)).astype(F32).astype(BF16)
    at = iota((4 * HERE, 4 * ROWS), 1)
    turn = (at >= ROWS).astype(jnp.int32) + (at >= 2 * ROWS).astype(jnp.int32) + (at >= 3 * ROWS).astype(jnp.int32)
    level = at - turn * ROWS
    source = ((z + turn) & 3) * HERE + level
    spread = ((iota((4 * HERE, 4 * ROWS), 0) == source) & (level < HERE)).astype(F32).astype(BF16)

    def chosen(part):
        rows = jnp.dot(pick, part, preferred_element_type=F32).astype(BF16)
        return jnp.dot(rows, spread, preferred_element_type=F32).astype(BF16)

    high, low = (chosen(part) for part in split(mix_ref[...]))
    both = jnp.concatenate([high.astype(F32), low.astype(F32)], axis=0).astype(BF16)
    pad = jnp.zeros((ROWS - HERE, 2 * LANES), F32)
    for s in range(2):
        rows = slice(s * HERE, (s + 1) * HERE)
        for sub in range(0, SUBS, 2):
            parts = []
            for d in range(4):
                parts += [jnp.concatenate([block(d, s * HERE, HERE, sub + i) for i in range(2)], axis=1), pad]
            x_high, x_low = split(jnp.concatenate(parts, axis=0))
            r = jnp.dot(both, x_high, preferred_element_type=F32)
            mixed = r[0:ROWS] + r[ROWS:] + jnp.dot(high, x_low, preferred_element_type=F32)
            for i in range(2):
                half = mixed[:, i * LANES : (i + 1) * LANES]
                field_ref[sub + i, s] = half
                out_ref[rows, sub + i, :] = half[0:HERE]
    for row in range(4):
        a, b, c, d = (weights(i, 2 * HERE + row) for i in range(4))
        number = (row * SUBS + iota((SUBS, LANES), 0)) * LANES + iota((SUBS, LANES), 1)
        scale_ref[row] = jnp.where(number < count_ref[0], 1.0 / ((a + c) + (b + d)), 0.0)


def place(own, rank):
    full = rank < LANES
    group = (own >> 2) * 3 + jnp.where(full, (own & 3) >> 1, 2)
    lane = jnp.where(full, (own & 1) * LANES + rank, (own & 3) * 64 + rank - LANES)
    return group, lane


def fetch(pairs, sem):
    copies = [pltpu.make_async_copy(a, b, sem.at[i]) for i, (a, b) in enumerate(pairs)]
    for copy in copies:
        copy.start()
    for copy in copies:
        copy.wait()


MESSAGE = 29
BOTH = 40


def send_kernel(
    kern_in, col_ref, own_ref, off_ref, part_ref, send_ref, place_ref, den_ref,
    kern_ref, w_ref, grp_ref, hot_ref, sem,
):
    weights = pltpu.make_async_copy(kern_in, kern_ref, sem)
    weights.start()
    before = (iota((WIDE, WIDE), 0) < iota((WIDE, WIDE), 1)).astype(BF16)
    slot = iota((WIDE, 1), 0)
    carry = jnp.zeros((TILES, 1), F32)
    for b in range(SND // WIDE):
        at = pl.ds(b * WIDE, WIDE)
        own = own_ref[:, at]
        onehot = (iota((TILES, WIDE), 0) == own).astype(F32)
        prefix = jnp.dot(onehot.astype(BF16), before, preferred_element_type=F32)
        rank = jnp.sum(onehot * (prefix + carry), axis=0, keepdims=True).astype(jnp.int32)
        carry = carry + jnp.sum(onehot, axis=1, keepdims=True)
        place_ref[:, at] = own * WIDE + rank
        group, lane = place(own, rank)
        grp_ref[:, at] = jnp.broadcast_to(group, (SUBS, WIDE))
        hot_ref[at, :] = (slot == lane).astype(F32).T.astype(BF16)

    weights.wait()
    z = lax.axis_index("lev")
    levels = z * HERE + iota((HERE, SND), 0)
    weighted = jnp.where(levels >= off_ref[...], kern_ref[...], 0.0)
    den = jnp.sum(weighted, axis=0, keepdims=True)
    for j in range(SND // LANES):
        den_ref[j // SUBS, j % SUBS : j % SUBS + 1, :] = den[:, j * LANES : (j + 1) * LANES]
    col = col_ref[...]
    high = weighted.astype(BF16).astype(F32)
    col_high = (col & ~3).astype(F32)
    last = slice(HERE - 2, HERE)
    w_ref[0:16, :] = high[0:16]
    w_ref[16:32, :] = (weighted - high)[0:16]
    w_ref[32:34, :] = high[last]
    w_ref[34:35, :] = col_high
    w_ref[35:37, :] = (weighted - high)[last]
    w_ref[37:38, :] = (col & 3).astype(F32)
    w_ref[38:40, :] = jnp.zeros((2, SND), F32)

    quads, chunk = 16, 1024
    sub, left = iota((SUBS, LANES), 0), iota((SUBS, LANES), 1) < 64

    def some(i):
        acc = jnp.zeros((quads * 3 * BOTH, WIDE), F32)
        for b in range(SND // chunk):
            at = pl.ds(b * chunk, chunk)
            w = w_ref[:, at]
            group = grp_ref[:, at]
            rows = []
            for j in range(quads * 3):
                here = group == i * quads * 3 + j
                rows += [jnp.where(here, w[k : k + SUBS], 0.0) for k in range(0, BOTH, SUBS)]
            lhs = jnp.concatenate(rows, axis=0).astype(BF16)
            acc = acc + jnp.dot(lhs, hot_ref[at, :], preferred_element_type=F32)
        for q in range(quads):
            sums = []
            for j in range(3):
                base = (q * 3 + j) * BOTH
                third = acc[base + 32 : base + 40]
                third = third + roll(third, 3 if j == 2 else -3, 0)
                sums.append((acc[base : base + 16] + acc[base + 16 : base + 32], third))
            for k in range(4):
                t = (i * quads + q) * 4 + k
                mine = slice((k % 2) * LANES, (k % 2 + 1) * LANES)
                pair = slice((k // 2) * LANES, (k // 2 + 1) * LANES)
                top, third = (x[:, mine] for x in sums[k // 2])
                rest, middle = (x[:, pair] for x in sums[2])
                if k % 2 == 0:
                    bottom = jnp.where(left, rest[0:8], roll(rest[8:16], 64, 1))
                else:
                    bottom = jnp.where(left, roll(rest[0:8], 64, 1), rest[8:16])
                    middle = roll(middle, 64, 1)
                send_ref[MESSAGE * t : MESSAGE * t + 16, :] = top
                send_ref[MESSAGE * t + 16 : MESSAGE * t + 24, :] = bottom
                after = roll(middle, -1, 0)
                split_row = jnp.where(left, middle, roll(after, 64, 1))
                tail = jnp.where(sub < 3, third, jnp.where(sub == 3, split_row, after))
                send_ref[MESSAGE * t + 24 : MESSAGE * t + 29, :] = tail[0:5]

    for i in range(TILES // (4 * quads)):
        some(i)


FIELD = 40


def sample_kernel(got_ref, field_ref, out_ref, f_ref):
    sub, lane = iota((SUBS, LANES), 0), iota((SUBS, LANES), 1)
    left = lane < 64
    for h in range(4):
        blocks = []
        for lon in range(2):
            x, y = field_ref[2 * h + lon, 0], field_ref[2 * h + lon, 1]
            third = jnp.where(sub < 2, x[16:24], roll(y[16:24], 3, 0))
            blocks.append(jnp.concatenate([x[0:16], y[0:16], third], axis=0))
        high, low = split(jnp.concatenate(blocks, axis=1))
        f_ref[h * FIELD : (h + 1) * FIELD, :] = high
        f_ref[(4 + h) * FIELD : (5 + h) * FIELD, :] = low
    spot = iota((WIDE, 1), 0)
    row = iota((SUBS, WIDE), 0)

    def sums(w, col):
        col = col.astype(jnp.int32)
        hot = (spot == (col & 127) + ((col >> 9) << 7)).astype(F32).astype(BF16)
        block = jnp.broadcast_to((col >> 7) & 3, (SUBS, WIDE))
        hits = [block == h for h in range(4)]
        both = jnp.dot(f_ref[...], hot, preferred_element_type=F32)
        values = both[0 : 4 * FIELD] + both[4 * FIELD :]

        def pick(base):
            out = values[base : base + 8]
            for h in range(1, 4):
                out = jnp.where(hits[h], values[h * FIELD + base : h * FIELD + base + 8], out)
            return out

        last = jnp.where(row < 2, w[2], 0.0)
        last = pick(32) * (last + roll(last, 3, 0))
        totals = []
        for s in range(2):
            total = pick(16 * s) * w[0] + pick(16 * s + 8) * w[1] + jnp.where((row < 3) == (s == 0), last, 0.0)
            totals.append(jnp.sum(total, axis=0, keepdims=True))
        return totals

    def wide(a, b):
        return jnp.concatenate([a, b], axis=1)

    def last_of(x, y):
        a = jnp.where(left, x, roll(y, 64, 1))
        b = jnp.where(left, roll(x, 64, 1), y)
        return jnp.where(sub == 0, roll(a, -3, 0), jnp.where(sub == 1, roll(b, -2, 0), roll(a, -2, 0)))

    quads = QUADS
    half = lane[0:1] < 64

    def some(i, _):
        rows = []
        step = 4 * quads * MESSAGE
        got = got_ref.at[pl.ds(pl.multiple_of(i * step, SUBS), step)]
        for q in range(quads):
            xs = []
            for k in range(4):
                base = (q * 4 + k) * MESSAGE
                tail = jnp.concatenate([got[base + 24 : base + 29, :], jnp.zeros((3, LANES), F32)], axis=0)
                xs.append([got[base : base + 8, :], got[base + 8 : base + 16, :], tail, got[base + 16 : base + 24, :]])
            results, rest = [], []
            for x, y in (xs[0:2], xs[2:4]):
                w = [wide(x[g], y[g]) for g in range(3)]
                results.append(sums(w, w[2][2:3]))
                rest.append(
                    (
                        jnp.where(left, x[3], roll(y[3], 64, 1)),
                        jnp.where(left, roll(x[3], 64, 1), y[3]),
                        last_of(x[2], y[2]),
                    )
                )
            w = [wide(rest[0][g], rest[1][g]) for g in range(3)]
            tails = sums(w, w[2][2:3])
            for k in range(4):
                mine = slice((k % 2) * LANES, (k % 2 + 1) * LANES)
                pair = slice((k // 2) * LANES, (k // 2 + 1) * LANES)
                a, b = tails[0][:, pair], tails[1][:, pair]
                tail = jnp.where(half, a, roll(b, 64, 1)) if k % 2 == 0 else jnp.where(half, roll(a, 64, 1), b)
                rows += [results[k // 2][0][:, mine], results[k // 2][1][:, mine], tail]
        size = 12 * quads
        out_ref[pl.ds(pl.multiple_of(i * size, SUBS), size), :] = jnp.concatenate(rows, axis=0)
        return 0

    lax.fori_loop(0, TILES // (4 * quads), some, 0)


def home_kernel(back_ref, place_ref, out_ref):
    plain, other, tail = (back_ref[pl.ds(j, TILES, stride=3), :] for j in range(3))
    first = jnp.concatenate([plain, tail], axis=1)
    second = jnp.concatenate([other, roll(tail, 64, 1)], axis=1)
    parts = jnp.concatenate(split(jnp.concatenate([first, second], axis=0)), axis=0)
    slot = iota((WIDE, 1), 0)
    for b in range(SND // WIDE):
        at = pl.ds(b * WIDE, WIDE)
        hot = (slot == (place_ref[:, at] & (WIDE - 1))).astype(F32).astype(BF16)
        both = jnp.dot(parts, hot, preferred_element_type=F32)
        values = both[0 : 2 * TILES] + both[2 * TILES :]
        mine = iota((TILES, WIDE), 0) == (place_ref[:, at] >> 8)
        for s in range(2):
            picked = jnp.where(mine, values[s * TILES : (s + 1) * TILES], 0.0)
            total = jnp.sum(picked, axis=0, keepdims=True)
            for i in range(2):
                j = s * 32 + 2 * b + i
                out_ref[j // SUBS, j % SUBS : j % SUBS + 1, :] = total[:, i * LANES : (i + 1) * LANES]


def last_kernel(a_ref, b_ref, d_ref, c_ref, scale_ref, out_ref):
    for row in range(4):
        scale = scale_ref[row]
        for s in range(2):
            k = s * 4 + row
            num = (a_ref[k] + c_ref[k]) + (b_ref[k] + d_ref[k])
            value = jnp.where(scale > 0, num * scale, 0.0)
            for j in range(SUBS):
                at = (row * SUBS + j) * LANES
                out_ref[s : s + 1, at : at + LANES] = value[j : j + 1]


def call(kernel, outs, in_specs, scratch=(), mib=12, flops=10**6, name=None):
    single = not isinstance(outs, (list, tuple))
    shapes = [outs] if single else outs
    return pl.pallas_call(
        kernel,
        out_shape=outs if single else list(outs),
        in_specs=in_specs,
        out_specs=spec() if single else [spec() for _ in shapes],
        scratch_shapes=list(scratch),
        compiler_params=params(mib),
        name=name,
        cost_estimate=pl.CostEstimate(flops=flops, bytes_accessed=10**5, transcendentals=0),
    )


def arr(shape, dtype=F32):
    return jax.ShapeDtypeStruct(shape, dtype)


def registers(x):
    rows = x.size // (SUBS * LANES)
    return x.reshape(rows, 2, 4, LANES).transpose(0, 2, 1, 3).reshape(rows, SUBS, LANES)


def swapped(x, start):
    size = lax.axis_size("tile")
    pairs = [((i + start) % size, (i + start + 1) % size) for i in range(0, size, 2)]
    return lax.ppermute(x, "tile", pairs + [(b, a) for a, b in pairs])


def far(x):
    return pltpu.with_memory_space_constraint(x, HBM)


def shift(x, axis, distance):
    size = lax.axis_size(axis)
    return lax.ppermute(x, axis, [(i, (i + distance) % size) for i in range(size)])


def body(tracer, u_courant, v_courant, surface_flux, mixing, kernel, column, owner_tile, offset, counts):
    c, u, v, f = (registers(x) for x in (tracer, u_courant, v_courant, surface_flux))
    col, own, off = (x.reshape(1, SND) for x in (column, owner_tile, offset))
    block = arr((2 * HERE, SUBS, LANES))
    near_half, far_half, part = call(
        halo_kernel,
        [arr((45, SUBS, LANES)), arr((45, SUBS, LANES)), block],
        [spec(HBM)] * 4,
        [
            pltpu.VMEM((2 * HERE, SUBS, LANES), F32),
            pltpu.VMEM((HERE, SUBS, LANES), F32),
            pltpu.VMEM((HERE, SUBS, LANES), F32),
            pltpu.VMEM((2, SUBS, LANES), F32),
            pltpu.SemaphoreType.DMA((4,)),
        ],
        name="halo",
    )(*(far(x) for x in (c, u, v, f)))
    from_near, from_far = swapped(near_half, 0), swapped(far_half, 1)
    send, place_of, den = call(
        send_kernel,
        [arr((TILES * MESSAGE, LANES)), arr((1, SND), jnp.int32), arr((4, SUBS, LANES))],
        [spec(HBM)] + [spec()] * 4,
        [pltpu.VMEM((HERE, SND), F32), pltpu.VMEM((BOTH, SND), F32), pltpu.VMEM((SUBS, SND), jnp.int32), pltpu.VMEM((SND, WIDE), BF16), pltpu.SemaphoreType.DMA],
        mib=28,
        flops=9 * 10**9,
        name="send",
    )(far(kernel), col, own, off, part)
    adv = call(advect_kernel, arr((40, SUBS, LANES)), [spec()] * 8, name="advect")(
        c, u, v, f, part, from_near, from_far, den
    )
    up, down = shift(adv, "lev", -1), shift(adv, "lev", 1)
    across = [shift(adv, "lev", 2)]
    mark = call(mark_kernel, arr((SUBS, LANES)), [spec()], name="mark")(adv)
    send, mark = lax.optimization_barrier((send, mark))
    got = lax.all_to_all(send.reshape(TILES, 1, MESSAGE * LANES), "tile", 0, 0, tiled=True)
    got = got.reshape(TILES * MESSAGE, LANES)
    transported, field, scale = call(
        mix_kernel,
        [block, arr((SUBS, 2, ROWS, LANES)), arr((4, SUBS, LANES))],
        [spec(SMEM)] + [spec()] * (5 + len(across)),
        flops=10**11,
        name="mix",
    )(counts, mixing, mark, adv, up, down, *across)
    sums = call(
        sample_kernel,
        arr((3 * TILES, LANES)),
        [spec()] * 2,
        [pltpu.VMEM((8 * FIELD, WIDE), BF16)],
        mib=24,
        name="sample",
    )(got, field)
    back = lax.all_to_all(sums.reshape(TILES, 1, 3 * LANES), "tile", 0, 0, tiled=True)
    back = back.reshape(3 * TILES, LANES)
    mine = call(home_kernel, arr((8, SUBS, LANES)), [spec()] * 2, name="home")(back, place_of)
    nums = [shift(mine, "lev", -d) for d in (1, 2, 3)]
    evolved = call(last_kernel, arr((2, SND)), [spec()] * 5, name="last")(mine, nums[0], nums[2], nums[1], scale)
    out = transported.reshape(2 * HERE, 4, 2, LANES).transpose(0, 2, 1, 3).reshape(tracer.shape)
    return out, evolved


def solution(mesh):
    in_specs = (
        P(None, "lev", "tile", None),
        P("lev", "tile", None),
        P("lev", "tile", None),
        P(None, "tile", None),
        P(),
        P("lev", "tile"),
        P("tile"),
        P("tile"),
        P("tile"),
        P("tile"),
    )
    out_specs = (P(None, "lev", "tile", None), P(None, "tile"))
    return jax.shard_map(body, mesh=mesh, in_specs=in_specs, out_specs=out_specs, check_vma=False)
```
